256 devices in a mesh: gx: 16 (over y, x), gy: 16 (over z, core).
Axes of the slice: x: 4, y: 4, z: 8, core: 2. Of those that a mesh axis runs over, the one named last changes fastest.
Arguments:
- atom_cell: int32 [16, 16, 4096], P('gx', 'gy'), may hold values from 0 to 49151
- atom_frac: float32 [3, 16, 16, 4096], P(None, 'gx', 'gy'), may hold values from 0 to 1
- atom_charge: float32 [16, 16, 4096], P('gx', 'gy'), may hold values from -6 to 6
- atom_count: int32 [16, 16], P('gx', 'gy'), may hold values from 1024 to 4096, as said below
- fine_kernel: float32 [9, 9, 9], replicated, may hold values from -1.8 to 1.8
- middle_kernel: float32 [9, 9, 9], replicated, may hold values from -0.9 to 0.9
- coarse_kernel: float32 [9, 9, 9], replicated, may hold values from -0.36 to 0.36
Outputs:
- potential: float32 [256, 384, 128], P('gx', 'gy')
- forces: float32 [3, 16, 16, 4096], P(None, 'gx', 'gy')
The draws below stay inside these ranges and needn't reach their ends.
Inputs may be any that keep to these rules, and one draw needn't show every extreme that they name: `atom_count`: slots at or past a block's count hold no atom. At least one block is full in every draw; about a quarter of the blocks are nearly full and the rest hold a quarter to a half of 4096.
All inputs are finite; a program needn't handle non-finite values.
Results may differ from the reference program's by a relative error of at most 0.0003.
Values sent between devices are 32-bit elements; how exact they have to be, the bound alone decides.
No kernel may reach another device: no remote copies, remote signals or barrier semaphores. Data moves between devices by JAX's collectives and lax.ppermute only.
A program may use at most 128 MiB of HBM per device.

```python
import jax
import jax.numpy as jnp
from jax import lax

CX = 16
CY = 24
NZ = 128
ATOMS_DEV = 4096
KERNEL = 9
NX = 256
NY = 384
N_GX = 16
N_GY = 16


def draw_atom_count(key, part):
    key_low = jax.random.fold_in(key, 11)
    key_high = jax.random.fold_in(key, 12)
    key_pick = jax.random.fold_in(key, 13)
    key_full = jax.random.fold_in(key, 14)
    light = jax.random.randint(key_low, (N_GX, N_GY), ATOMS_DEV // 4, ATOMS_DEV // 2 + 1)
    heavy = ATOMS_DEV - jax.random.randint(key_high, (N_GX, N_GY), 0, ATOMS_DEV // 8)
    chosen = jax.random.randint(key_pick, (N_GX, N_GY), 0, 4) == 0
    counts = jnp.where(chosen, heavy, light).reshape(-1)
    fullest = jax.random.randint(key_full, (), 0, N_GX * N_GY)
    counts = jnp.where(jnp.arange(N_GX * N_GY) == fullest, ATOMS_DEV, counts)
    return counts.reshape(N_GX, N_GY).astype(jnp.int32)


def set_ends(entries, rng, least, high):
    spot = [jax.random.randint(jax.random.fold_in(rng, axis), (), 0, length) for axis, length in enumerate(entries.shape)]
    main_axis = entries.shape.index(max(entries.shape))
    next_to = spot[:main_axis] + [(spot[main_axis] + 1) % entries.shape[main_axis]] + spot[main_axis + 1:]
    return entries.at[tuple(spot)].set(least).at[tuple(next_to)].set(high)


def block_scale(own_key, extent, shards, least, high):
    gain, own = 1.0, jax.random.fold_in(own_key, 6)
    for axis_at, blocks in shards:
        steps = jnp.exp(jax.random.uniform(jax.random.fold_in(own, axis_at), (blocks,), jnp.float32, least / len(shards), high / len(shards)))
        gain = gain * jnp.repeat(steps, extent[axis_at] // blocks).reshape([-1 if axis == axis_at else 1 for axis in range(len(extent))])
    return gain


def normal_values(stream_key, shape, spread, reach, split=(), held_as=jnp.bfloat16):
    result = jax.random.normal(stream_key, shape, jnp.float32) * spread
    if len(split) > 0:
        result = block_scale(stream_key, shape, split, -0.22, 0.18) * result
    return jnp.clip(result, min=-reach, max=reach).astype(held_as)


def setup_inputs(seed: int = 0) -> dict:
    keys = jax.random.split(jax.random.key(seed), 8)
    atom_cell = set_ends(jax.random.randint(keys[0], (N_GX, N_GY, ATOMS_DEV), 0, CX * CY * NZ), jax.random.fold_in(keys[0], 1), 0, (CX * CY * NZ) - 1).astype(jnp.int32)
    atom_frac = jnp.clip(1.0 * jax.random.uniform(keys[1], (3, N_GX, N_GY, ATOMS_DEV), jnp.float32) ** block_scale(keys[1], (3, N_GX, N_GY, ATOMS_DEV), ((1, 16), (2, 16)), -0.2, 0.2), 0.0, 1.0)
    atom_charge = normal_values(keys[2], (N_GX, N_GY, ATOMS_DEV), 1.0, 6.0, ((0, 16), (1, 16)), jnp.float32)
    atom_count = draw_atom_count(jax.random.fold_in(keys[7], 71), 0)
    fine_kernel = normal_values(keys[4], (KERNEL, KERNEL, KERNEL), 0.3, 1.8, (), jnp.float32)
    middle_kernel = normal_values(keys[5], (KERNEL, KERNEL, KERNEL), 0.15, 0.9, (), jnp.float32)
    coarse_kernel = normal_values(keys[6], (KERNEL, KERNEL, KERNEL), 0.06, 0.36, (), jnp.float32)
    return dict(atom_cell=atom_cell, atom_frac=atom_frac, atom_charge=atom_charge, atom_count=atom_count, fine_kernel=fine_kernel, middle_kernel=middle_kernel, coarse_kernel=coarse_kernel)


def kernel_grid(kernel, grid_shape):
    half_width = KERNEL // 2
    offsets = jnp.arange(KERNEL, dtype=jnp.int32)
    place_x = jnp.mod(half_width - offsets, grid_shape[0])
    place_y = jnp.mod(half_width - offsets, grid_shape[1])
    place_z = jnp.mod(half_width - offsets, grid_shape[2])
    empty = jnp.zeros(grid_shape, jnp.float32)
    return empty.at[place_x[:, None, None], place_y[None, :, None], place_z[None, None, :]].add(kernel)


def convolve_whole(grid_in, kernel):
    spectrum = jnp.fft.rfftn(grid_in) * jnp.fft.rfftn(kernel_grid(kernel, grid_in.shape).astype(grid_in.dtype))
    return jnp.fft.irfftn(spectrum, s=grid_in.shape).astype(grid_in.dtype)


def restrict_whole(grid_in):
    for dimension in range(3):
        grid_in = 0.5 * jnp.roll(grid_in, 1, dimension) + grid_in + 0.5 * jnp.roll(grid_in, -1, dimension)
        grid_in = lax.slice_in_dim(grid_in, 0, grid_in.shape[dimension], 2, dimension)
    return grid_in


def prolong_whole(grid_in):
    for dimension in range(3):
        paired = jnp.stack([grid_in, 0.5 * (grid_in + jnp.roll(grid_in, -1, dimension))], axis=dimension + 1)
        new_shape = list(grid_in.shape)
        new_shape[dimension] = 2 * new_shape[dimension]
        grid_in = paired.reshape(new_shape)
    return grid_in


def reference(atom_cell, atom_frac, atom_charge, atom_count, fine_kernel, middle_kernel, coarse_kernel):
    block_x = jnp.arange(N_GX, dtype=jnp.int32)[:, None, None]
    block_y = jnp.arange(N_GY, dtype=jnp.int32)[None, :, None]
    base_x = block_x * CX + atom_cell // (CY * NZ)
    base_y = block_y * CY + (atom_cell // NZ) % CY
    base_z = atom_cell % NZ
    slot_index = jnp.arange(ATOMS_DEV, dtype=jnp.int32)[None, None, :]
    is_live = slot_index < atom_count[:, :, None]
    live_charge = jnp.where(is_live, atom_charge, 0.0)
    corner_ids = []
    weights = []
    slopes = []
    for corner in range(8):
        raised = [(corner >> 2) & 1, (corner >> 1) & 1, corner & 1]
        factors = [atom_frac[dimension] if raised[dimension] else 1.0 - atom_frac[dimension] for dimension in range(3)]
        sign_list = [1.0 if raised[dimension] else -1.0 for dimension in range(3)]
        flat_index = ((base_x + raised[0]) % NX * NY + (base_y + raised[1]) % NY) * NZ + (base_z + raised[2]) % NZ
        corner_ids.append(flat_index.astype(jnp.int32))
        weights.append(factors[0] * factors[1] * factors[2])
        slopes.append(jnp.stack([sign_list[0] * factors[1] * factors[2], factors[0] * sign_list[1] * factors[2], factors[0] * factors[1] * sign_list[2]]))
    corner_ids = jnp.stack(corner_ids)
    weights = jnp.stack(weights)
    spread_values = weights * live_charge[None]
    fine_charge = jax.ops.segment_sum(spread_values.reshape(-1), corner_ids.reshape(-1), num_segments=NX * NY * NZ).reshape(NX, NY, NZ)
    middle_charge = restrict_whole(fine_charge)
    coarse_charge = restrict_whole(middle_charge)
    coarse_potential = convolve_whole(coarse_charge, coarse_kernel)
    middle_potential = convolve_whole(middle_charge, middle_kernel) + prolong_whole(coarse_potential)
    potential = convolve_whole(fine_charge, fine_kernel) + prolong_whole(middle_potential)
    flat_potential = potential.reshape(-1)
    running = jnp.zeros((3, N_GX, N_GY, ATOMS_DEV), potential.dtype)
    for corner in range(8):
        running = running + slopes[corner] * flat_potential[corner_ids[corner]][None]
    forces = -live_charge[None] * running
    return potential, forces
```

```python
import functools

import jax
import jax.numpy as jnp
import numpy as np
from jax import lax
from jax.experimental import pallas as pl
from jax.experimental.pallas import tpu as pltpu
from jax.sharding import PartitionSpec as P

CX = 16
CY = 24
NZ = 128
ATOMS = 4096
KERNEL = 9
TILE = 512
HIGHEST = lax.Precision.HIGHEST
F32 = jnp.float32
BF16 = jnp.bfloat16
VMEM_LIMIT = 48 * 1024 * 1024


def lanes_of(n, first):
    half = n // 2
    real = [(first + k, k) for k in range(half)]
    imag = [(first + 64 + k, k) for k in range(1, half)]
    return real, imag, first + 64


def forward_table(n, first):
    z = np.arange(n)
    out = np.zeros((n, 128))
    real, imag, top = lanes_of(n, first)
    for lane, k in real:
        out[:, lane] = np.cos(2 * np.pi * k * z / n)
    for lane, k in imag:
        out[:, lane] = -np.sin(2 * np.pi * k * z / n)
    out[:, top] = np.cos(np.pi * z)
    return out


def inverse_table(n, first):
    z = np.arange(n)
    out = np.zeros((128, n))
    real, imag, top = lanes_of(n, first)
    for lane, k in real:
        out[lane] = (1 if k == 0 else 2) / n * np.cos(2 * np.pi * k * z / n)
    for lane, k in imag:
        out[lane] = -2 / n * np.sin(2 * np.pi * k * z / n)
    out[top] = np.cos(np.pi * z) / n
    return out


def tap_tables(n, first):
    c = np.arange(KERNEL) - KERNEL // 2
    direct = np.zeros((KERNEL, 128))
    crossed = np.zeros((KERNEL, 128))
    real, imag, top = lanes_of(n, first)
    for lane, k in real:
        direct[:, lane] = np.cos(2 * np.pi * k * c / n)
        crossed[:, lane] = -np.sin(2 * np.pi * k * c / n)
    for lane, k in imag:
        direct[:, lane] = np.cos(2 * np.pi * k * c / n)
        crossed[:, lane] = np.sin(2 * np.pi * k * c / n)
    direct[:, top] = np.cos(np.pi * c)
    return np.concatenate([direct, crossed], axis=1)


def restrict_z(n):
    out = np.zeros((n, n // 2))
    for i in range(n // 2):
        out[(2 * i - 1) % n, i] += 0.5
        out[2 * i, i] += 1.0
        out[(2 * i + 1) % n, i] += 0.5
    return out


def prolong_z(n):
    return restrict_z(2 * n).T


def tents(fine, step, coarse):
    far = np.abs(np.arange(fine)[None, :] - step * np.arange(coarse)[:, None])
    return np.maximum(0.0, 1.0 - far / step)


def plane_table(step):
    cx, cy = CX // step + 1, CY // step + 1
    along_x = tents(CX + 1, step, cx)
    along_y = tents(CY + 1, step, cy)
    out = np.zeros((9, 16, CX + 1, 32))
    out[:cx, :cy, :, : CY + 1] = along_x[:, None, :, None] * along_y[None, :, None, :]
    return out.reshape(144, (CX + 1) * 32)


def tables():
    planes = np.concatenate([plane_table(2), plane_table(4)], axis=0)
    forward = np.stack(
        [
            forward_table(128, 0),
            restrict_z(128) @ forward_table(64, 0),
            restrict_z(128) @ restrict_z(64) @ forward_table(32, 32),
        ]
    )
    inverse = np.stack(
        [
            inverse_table(128, 0),
            inverse_table(64, 0) @ prolong_z(64),
            inverse_table(32, 32) @ prolong_z(32) @ prolong_z(64),
        ]
    )
    taps = np.stack([tap_tables(128, 0), tap_tables(64, 0), tap_tables(32, 32)])
    return [np.asarray(t, np.float32) for t in (planes, planes.T, forward, inverse, taps)]


def dot(a, b):
    return jnp.dot(a, b, precision=HIGHEST, preferred_element_type=F32)


def split(value):
    high = value.astype(BF16)
    return high, (value - high.astype(F32)).astype(BF16)


def coarse_lanes(shape):
    lane = lax.broadcasted_iota(jnp.int32, shape, len(shape) - 1) % 64
    return lane >= 32


def rows_of(cell_ref, frac_ref, charge_ref, count_ref, t):
    span = pl.ds(t * TILE, TILE)
    cell = cell_ref[0, :, span]
    f = [frac_ref[k, 0, :, span] for k in range(3)]
    slot = lax.broadcasted_iota(jnp.int32, (1, TILE), 1) + t * TILE
    charge = jnp.where(slot < count_ref[0, 0], charge_ref[0, :, span], 0.0)
    return cell, f, charge, span


def one_hot(cell):
    row = lax.broadcasted_iota(jnp.int32, (CX * CY, TILE), 0)
    return jnp.where(row == (cell >> 7), 1.0, 0.0).astype(BF16)


def spread_kernel(
    count_ref, par_ref, cell_ref, frac_ref, charge_ref, planes_ref, forward_ref,
    shat_ref, mc_ref, s1_ref, s2_ref, t1_ref, t2_ref, acc_ref, grid_ref,
):
    acc_ref[...] = jnp.zeros_like(acc_ref)

    def step(t, carry):
        cell, f, charge, _ = rows_of(cell_ref, frac_ref, charge_ref, count_ref, t)
        hot = one_hot(cell)
        z = cell & (NZ - 1)
        plane = lax.broadcasted_iota(jnp.int32, (NZ, TILE), 0)
        at_low = plane == z
        at_high = plane == ((z + 1) & (NZ - 1))
        wx = [1.0 - f[0], f[0]]
        wy = [1.0 - f[1], f[1]]
        wz = [1.0 - f[2], f[2]]
        for ab in range(4):
            flat = charge * wx[ab >> 1] * wy[ab & 1]
            value = jnp.where(at_low, flat * wz[0], jnp.where(at_high, flat * wz[1], 0.0))
            high, low = split(value)
            dims = (((1,), (1,)), ((), ()))
            acc_ref[:, ab * NZ : (ab + 1) * NZ] += lax.dot_general(
                hot, high, dims, preferred_element_type=F32
            ) + lax.dot_general(hot, low, dims, preferred_element_type=F32)
        return carry

    lax.fori_loop(0, ATOMS // TILE, step, 0)
    grid_ref[...] = jnp.zeros_like(grid_ref)
    for ab in range(4):
        a, b = ab >> 1, ab & 1
        for x in range(CX):
            grid_ref[x + a, b : b + CY, :] += acc_ref[
                x * CY : (x + 1) * CY, ab * NZ : (ab + 1) * NZ
            ]
    grid = grid_ref[...].reshape((CX + 1) * 32, NZ)
    shat = dot(grid, forward_ref[0])
    shat_ref[...] = shat.reshape(CX + 1, 32, NZ)
    small = dot(planes_ref[...], grid)
    mc = dot(small[:144], forward_ref[1]) + dot(small[144:], forward_ref[2])
    mc_ref[...] = mc.reshape(9, 16, NZ)

    even = par_ref[0] == 0
    even2 = par_ref[1] == 0
    is_coarse = coarse_lanes((5, 16, NZ))

    def put_low(ref):
        ref[:, :32, :] = shat_ref[0:5]
        ref[:, 32:, :] = mc_ref[0:5]

    def put_high(ref):
        ref[:, :32, :] = shat_ref[12:17]
        ref[:, 32:, :] = jnp.where(is_coarse, mc_ref[0:5], mc_ref[4:9])

    @pl.when(even)
    def _():
        put_high(s1_ref)
        put_low(s2_ref)

    @pl.when(jnp.logical_not(even))
    def _():
        put_low(s1_ref)
        put_high(s2_ref)

    @pl.when(even2)
    def _():
        t1_ref[...] = mc_ref[4]
        t2_ref[...] = mc_ref[0]

    @pl.when(jnp.logical_not(even2))
    def _():
        t1_ref[...] = mc_ref[0]
        t2_ref[...] = mc_ref[4]


def taps_kernel(fine_ref, middle_ref, coarse_ref, taps_ref, pq_ref, pqm_ref):
    for a in range(KERNEL):
        pq_ref[a] = dot(fine_ref[a], taps_ref[0])
        pqm_ref[a] = dot(middle_ref[a], taps_ref[1]) + dot(coarse_ref[a], taps_ref[2])


def merge_kernel(
    par_ref, shat_ref, mc_ref, r1_ref, r2_ref, rt1_ref, rt2_ref,
    e_ref, g_ref, s1_ref, s2_ref,
):
    e_ref[0:4] = jnp.zeros((4, 32, NZ), F32)
    e_ref[21:25] = jnp.zeros((4, 32, NZ), F32)
    e_ref[4:21] = shat_ref[...]
    g_ref[0:4] = jnp.zeros((4, 16, NZ), F32)
    g_ref[13:17] = jnp.zeros((4, 16, NZ), F32)
    g_ref[4:13] = mc_ref[...]
    is_coarse = coarse_lanes((5, 16, NZ))

    def merge(low_ref, high_ref):
        e_ref[0:5] += low_ref[:, :32, :]
        e_ref[20:25] += high_ref[:, :32, :]
        g_ref[0:5] += low_ref[:, 32:, :]
        high = high_ref[:, 32:, :]
        g_ref[12:17] += jnp.where(is_coarse, 0.0, high)
        g_ref[8:13] += jnp.where(is_coarse, high, 0.0)

    def merge2(low_ref, high_ref):
        g_ref[0] += jnp.where(is_coarse[0], low_ref[...], 0.0)
        g_ref[12] += jnp.where(is_coarse[0], high_ref[...], 0.0)

    even = par_ref[0] == 0
    even2 = par_ref[1] == 0

    @pl.when(even)
    def _():
        merge(r2_ref, r1_ref)

    @pl.when(jnp.logical_not(even))
    def _():
        merge(r1_ref, r2_ref)

    @pl.when(even2)
    def _():
        merge2(rt2_ref, rt1_ref)

    @pl.when(jnp.logical_not(even2))
    def _():
        merge2(rt1_ref, rt2_ref)

    def put_low(ref):
        ref[0:25] = e_ref[:, 0:8, :]
        ref[25:42] = g_ref[:, 0:8, :]

    def put_high(ref):
        ref[0:25, 0:5, :] = e_ref[:, 20:25, :]
        ref[0:25, 5:8, :] = jnp.zeros((25, 3, NZ), F32)
        ref[25:42] = jnp.where(
            coarse_lanes((17, 8, NZ)), g_ref[:, 2:10, :], g_ref[:, 8:16, :]
        )

    y_even = par_ref[2] == 0

    @pl.when(y_even)
    def _():
        put_high(s1_ref)
        put_low(s2_ref)

    @pl.when(jnp.logical_not(y_even))
    def _():
        put_low(s1_ref)
        put_high(s2_ref)


def finish_kernel(
    count_ref, par_ref, e_ref, g_ref, r1_ref, r2_ref, pq_ref, pqm_ref,
    cell_ref, frac_ref, charge_ref, planes_ref, inverse_ref,
    pot_ref, force_ref,
    ee_ref, es_ref, gg_ref, gs_ref, bpq_ref, bpqm_ref, out_ref, outm_ref, full_ref, turned_ref,
):
    for ref, wide, src in ((ee_ref, 32, e_ref), (gg_ref, 16, g_ref)):
        ref[:, 0:4, :] = jnp.zeros((ref.shape[0], 4, NZ), F32)
        ref[:, 4 + wide :, :] = jnp.zeros((ref.shape[0], 4, NZ), F32)
        ref[:, 4 : 4 + wide, :] = src[...]
    is_coarse = coarse_lanes((17, 5, NZ))

    def merge(low_ref, high_ref):
        ee_ref[:, 0:5, :] += low_ref[0:25, 0:5, :]
        ee_ref[:, 28:33, :] += high_ref[0:25, 0:5, :]
        gg_ref[:, 0:5, :] += low_ref[25:42, 0:5, :]
        high = high_ref[25:42, 0:5, :]
        gg_ref[:, 16:21, :] += jnp.where(is_coarse, 0.0, high)
        gg_ref[:, 10:15, :] += jnp.where(is_coarse, high, 0.0)

    y_even = par_ref[2] == 0

    @pl.when(y_even)
    def _():
        merge(r2_ref, r1_ref)

    @pl.when(jnp.logical_not(y_even))
    def _():
        merge(r1_ref, r2_ref)

    es_ref[...] = pltpu.roll(ee_ref[...].reshape(25 * 40, NZ), 64, 1).reshape(25, 40, NZ)
    gs_ref[...] = pltpu.roll(gg_ref[...].reshape(17 * 24, NZ), 64, 1).reshape(17, 24, NZ)
    for a in range(KERNEL):
        for b in range(KERNEL):
            for dst, src in ((bpq_ref, pq_ref), (bpqm_ref, pqm_ref)):
                for half in range(2):
                    dst[a, b, half] = jnp.broadcast_to(
                        src[a, b : b + 1, half * NZ : (half + 1) * NZ], (8, NZ)
                    )

    def correlate(v_ref, vs_ref, taps, dst_ref, rows, tiles):
        def step(t, carry):
            acc = [jnp.zeros((8, NZ), F32) for _ in range(rows)]
            for b in range(KERNEL):
                for xin in range(rows + KERNEL - 1):
                    v = v_ref[xin, pl.ds(t * 8 + b, 8), :]
                    vs = vs_ref[xin, pl.ds(t * 8 + b, 8), :]
                    for a in range(KERNEL):
                        x = xin - a
                        if 0 <= x < rows:
                            acc[x] = acc[x] + v * taps[a, b, 0] + vs * taps[a, b, 1]
            for x in range(rows):
                dst_ref[x, pl.ds(t * 8, 8), :] = acc[x]
            return carry

        lax.fori_loop(0, tiles, step, 0)

    correlate(ee_ref, es_ref, bpq_ref, out_ref, CX + 1, 4)
    correlate(gg_ref, gs_ref, bpqm_ref, outm_ref, 9, 2)

    small = outm_ref[...].reshape(144, NZ)
    levels = jnp.concatenate([dot(small, inverse_ref[1]), dot(small, inverse_ref[2])], axis=0)
    full = dot(out_ref[...].reshape((CX + 1) * 32, NZ), inverse_ref[0]) + dot(
        planes_ref[...], levels
    )
    full_ref[...] = full.reshape(CX + 1, 32, NZ)
    pot_ref[...] = full_ref[0:CX, 0:CY, :]
    for ab in range(4):
        a, b = ab >> 1, ab & 1
        part = full_ref[a : a + CX, b : b + CY, :].reshape(CX * CY, NZ).T
        high, low = split(part)
        turned_ref[0, ab * NZ : (ab + 1) * NZ, :] = high
        turned_ref[1, ab * NZ : (ab + 1) * NZ, :] = low

    def step(t, carry):
        cell, f, charge, span = rows_of(cell_ref, frac_ref, charge_ref, count_ref, t)
        hot = one_hot(cell)
        z = cell & (NZ - 1)
        plane = lax.broadcasted_iota(jnp.int32, (NZ, TILE), 0)
        at_low = plane == z
        at_high = plane == ((z + 1) & (NZ - 1))
        corner = []
        for ab in range(4):
            rows = slice(ab * NZ, (ab + 1) * NZ)
            found = jnp.dot(turned_ref[0, rows, :], hot, preferred_element_type=F32) + jnp.dot(
                turned_ref[1, rows, :], hot, preferred_element_type=F32
            )
            corner.append(
                [
                    jnp.sum(jnp.where(mask, found, 0.0), axis=0, keepdims=True)
                    for mask in (at_low, at_high)
                ]
            )
        wx = [1.0 - f[0], f[0]]
        wy = [1.0 - f[1], f[1]]
        wz = [1.0 - f[2], f[2]]
        sign = [-1.0, 1.0]
        sums = [0.0, 0.0, 0.0]
        for a in range(2):
            for b in range(2):
                for e in range(2):
                    v = corner[2 * a + b][e]
                    sums[0] = sums[0] + sign[a] * wy[b] * wz[e] * v
                    sums[1] = sums[1] + wx[a] * sign[b] * wz[e] * v
                    sums[2] = sums[2] + wx[a] * wy[b] * sign[e] * v
        for k in range(3):
            force_ref[k, 0, :, span] = -charge * sums[k]
        return carry

    lax.fori_loop(0, ATOMS // TILE, step, 0)


def call(kernel, outs, args, in_smem, scratch=()):
    return pl.pallas_call(
        kernel,
        out_shape=[jax.ShapeDtypeStruct(shape, F32) for shape in outs],
        in_specs=[
            pl.BlockSpec(memory_space=pltpu.SMEM if k < in_smem else pltpu.VMEM)
            for k in range(len(args))
        ],
        out_specs=[pl.BlockSpec(memory_space=pltpu.VMEM) for _ in outs],
        scratch_shapes=list(scratch),
        compiler_params=pltpu.CompilerParams(vmem_limit_bytes=VMEM_LIMIT),
    )(*args)


def swap(value, axis, first, gap):
    pairs = []
    for i in range(16):
        partner = ((((i - first) % 16) ^ gap) + first) % 16
        pairs.append((i, partner))
    return lax.ppermute(value, axis, pairs)


def per_device(cell, frac, charge, count, fine, middle, coarse):
    planes, planes_t, forward, inverse, taps = (jnp.asarray(t) for t in tables())
    ix, iy = lax.axis_index("gx"), lax.axis_index("gy")
    par = jnp.stack([ix & 1, (ix >> 1) & 1, iy & 1]).astype(jnp.int32)
    shat, mc, s1, s2, t1, t2 = call(
        spread_kernel,
        [(17, 32, NZ), (9, 16, NZ), (5, 48, NZ), (5, 48, NZ), (16, NZ), (16, NZ)],
        (count, par, cell, frac, charge, planes, forward),
        2,
        [pltpu.VMEM((CX * CY, 4 * NZ), F32), pltpu.VMEM((17, 32, NZ), F32)],
    )
    r1 = swap(s1, "gx", 0, 1)
    r2 = swap(s2, "gx", 1, 1)
    rt1 = swap(t1, "gx", 0, 2)
    rt2 = swap(t2, "gx", 2, 2)
    pq, pqm = call(taps_kernel, [(9, 9, 2 * NZ), (9, 9, 2 * NZ)], (fine, middle, coarse, taps), 0)
    e, g, y1, y2 = call(
        merge_kernel,
        [(25, 32, NZ), (17, 16, NZ), (42, 8, NZ), (42, 8, NZ)],
        (par, shat, mc, r1, r2, rt1, rt2),
        1,
    )
    q1 = swap(y1, "gy", 0, 1)
    q2 = swap(y2, "gy", 1, 1)
    pot, force = call(
        finish_kernel,
        [(CX, CY, NZ), (3, 1, 1, ATOMS)],
        (count, par, e, g, q1, q2, pq, pqm, cell, frac, charge, planes_t, inverse),
        2,
        [
            pltpu.VMEM((25, 40, NZ), F32),
            pltpu.VMEM((25, 40, NZ), F32),
            pltpu.VMEM((17, 24, NZ), F32),
            pltpu.VMEM((17, 24, NZ), F32),
            pltpu.VMEM((9, 9, 2, 8, NZ), F32),
            pltpu.VMEM((9, 9, 2, 8, NZ), F32),
            pltpu.VMEM((17, 32, NZ), F32),
            pltpu.VMEM((9, 16, NZ), F32),
            pltpu.VMEM((17, 32, NZ), F32),
            pltpu.VMEM((2, 4 * NZ, CX * CY), BF16),
        ],
    )
    return pot, force


def solution(mesh):
    return jax.shard_map(
        per_device,
        mesh=mesh,
        in_specs=(
            P("gx", "gy", None),
            P(None, "gx", "gy", None),
            P("gx", "gy", None),
            P("gx", "gy"),
            P(),
            P(),
            P(),
        ),
        out_specs=(P("gx", "gy", None), P(None, "gx", "gy", None)),
        check_vma=False,
    )
```

```python
import functools

import jax
import jax.numpy as jnp
import numpy as np
from jax import lax
from jax.experimental import pallas as pl
from jax.experimental.pallas import tpu as pltpu
from jax.sharding import PartitionSpec as P

CX = 16
CY = 24
NZ = 128
ATOMS = 4096
KERNEL = 9
TILE = 1024
HIGHEST = lax.Precision.HIGHEST
F32 = jnp.float32
BF16 = jnp.bfloat16
VMEM_LIMIT = 48 * 1024 * 1024


LINE = CY + KERNEL
FIRST = {128: 0, 64: 65, 32: 98}


def forward_table(n):
    z, k = np.arange(n)[:, None], np.arange(n // 2 + 1)[None, :]
    turn = np.exp(-2j * np.pi * k * z / n)
    return placed(turn, n)


def placed(turn, n):
    out = np.zeros((turn.shape[0], 256))
    first, count = FIRST[n], n // 2 + 1
    out[:, first : first + count] = turn.real
    out[:, 128 + first : 128 + first + count] = turn.imag
    return out


def inverse_table(n):
    z, k = np.arange(n)[:, None], np.arange(n // 2 + 1)[None, :]
    weight = np.where((k == 0) | (k == n // 2), 1.0, 2.0) / n
    return placed(weight * np.exp(-2j * np.pi * k * z / n), n).T


def tap_tables(n):
    c, k = np.arange(KERNEL)[:, None] - KERNEL // 2, np.arange(n // 2 + 1)[None, :]
    return placed(np.exp(2j * np.pi * k * c / n), n)


def line_tables():
    k = np.arange(LINE)
    forward = np.zeros((40, 40), complex)
    forward[:LINE, :LINE] = np.exp(-2j * np.pi * np.outer(k, k) / LINE)
    back = np.zeros((32, 40), complex)
    back[: CY + 1, :LINE] = np.exp(2j * np.pi * np.outer(np.arange(CY + 1), k) / LINE) / LINE
    spread = np.zeros((40, KERNEL), complex)
    spread[:LINE] = np.exp(2j * np.pi * np.outer(k, np.arange(KERNEL)) / LINE)

    def both(table, copies):
        return np.concatenate(
            [np.kron(np.eye(copies), table.real), np.kron(np.eye(copies), table.imag)], axis=0
        )

    return both(forward, 5), both(back, 6), both(spread, 1)


def restrict_z(n):
    out = np.zeros((n, n // 2))
    for i in range(n // 2):
        out[(2 * i - 1) % n, i] += 0.5
        out[2 * i, i] += 1.0
        out[(2 * i + 1) % n, i] += 0.5
    return out


def prolong_z(n):
    return restrict_z(2 * n).T


def tents(fine, step, coarse):
    far = np.abs(np.arange(fine)[None, :] - step * np.arange(coarse)[:, None])
    return np.maximum(0.0, 1.0 - far / step)


def plane_table(step):
    cx, cy = CX // step + 1, CY // step + 1
    along_x = tents(CX + 1, step, cx)
    along_y = tents(CY + 1, step, cy)
    out = np.zeros((9, 16, CX + 1, 32))
    out[:cx, :cy, :, : CY + 1] = along_x[:, None, :, None] * along_y[None, :, None, :]
    return out.reshape(144, (CX + 1) * 32)


def halves(table):
    table = np.asarray(table, np.float32)
    high = table.astype(BF16)
    return np.stack([high, (table - high.astype(np.float32)).astype(BF16)])


def tables():
    small = np.zeros((128, 256))
    small[:64] = forward_table(64)
    small[64:96] = forward_table(32)
    line, back, spread = line_tables()
    inverse = np.concatenate(
        [
            inverse_table(64) @ prolong_z(64),
            inverse_table(32) @ prolong_z(32) @ prolong_z(64),
        ],
        axis=1,
    )
    parts = {
        "plane2": np.asarray(plane_table(2).T, BF16),
        "plane4": np.asarray(plane_table(4).T, BF16),
    }
    for name, table in (
        ("forward", forward_table(128)),
        ("small", small),
        ("line", line),
        ("back", back),
        ("inverse", inverse_table(128)),
        ("levels", inverse),
        ("spread", spread),
        ("tap128", tap_tables(128)),
        ("tap64", tap_tables(64)),
        ("tap32", tap_tables(32)),
    ):
        parts[name + "_high"], parts[name + "_low"] = halves(table)
    places = {}
    blocks = []
    start = 0
    for name, part in parts.items():
        rows, cols = part.shape
        whole = -(-rows // 16) * 16
        places[name] = (start, whole, cols)
        blocks.append(np.pad(part, ((0, whole - rows), (0, 256 - cols))))
        start += whole
    return np.concatenate(blocks, axis=0), places


PACKED, PLACES = tables()


def table(ref, name, first=0):
    if name + "_high" in PLACES:
        return table(ref, name + "_high", first), table(ref, name + "_low", first)
    start, rows, cols = PLACES[name]
    return ref[start - first : start - first + rows, :cols]


def whole(ref, name, first):
    high, low = table(ref, name, first)
    return high.astype(F32) + low.astype(F32)


def dot(a, b):
    return jnp.dot(a, b, precision=HIGHEST, preferred_element_type=F32)


def dot_exact(table, value):
    high, low = split(value)
    return jnp.dot(table, high, preferred_element_type=F32) + jnp.dot(
        table, low, preferred_element_type=F32
    )


def split(value):
    high = value.astype(BF16)
    return high, (value - high.astype(F32)).astype(BF16)


def dot3(a, b):
    total = jnp.dot(a[0], b[0], preferred_element_type=F32)
    total += jnp.dot(a[0], b[1], preferred_element_type=F32)
    return total + jnp.dot(a[1], b[0], preferred_element_type=F32)


def tent(far, step):
    return jnp.maximum(step - jnp.abs(far), 0)


def plane_tents(step):
    row = lax.broadcasted_iota(jnp.int32, (144, (CX + 1) * 32), 0)
    col = lax.broadcasted_iota(jnp.int32, (144, (CX + 1) * 32), 1)
    along_x = tent((col >> 5) - step * (row >> 4), step)
    along_y = tent((col & 31) - step * (row & 15), step)
    return ((along_x * along_y).astype(F32) * (1.0 / step**2)).astype(BF16)


def depth_tents(step, first):
    row = lax.broadcasted_iota(jnp.int32, (NZ, NZ), 0)
    col = lax.broadcasted_iota(jnp.int32, (NZ, NZ), 1) - first
    far = (row - step * col) & (NZ - 1)
    weight = tent(far, step) + tent(NZ - far, step)
    weight = jnp.where((col >= 0) & (col < NZ // step), weight, 0)
    return (weight.astype(F32) * (1.0 / step)).astype(BF16)


def dot_right(value, table):
    high, low = split(value)
    return jnp.dot(high, table, preferred_element_type=F32) + jnp.dot(
        low, table, preferred_element_type=F32
    )


def coarse_lanes(shape):
    return lax.broadcasted_iota(jnp.int32, shape, len(shape) - 1) >= 64


def rows_of(cell_ref, frac_ref, charge_ref, t):
    span = pl.ds(t * TILE, TILE)
    cell = cell_ref[0, :, span]
    f = [frac_ref[k, 0, :, span] for k in range(3)]
    return cell, f, charge_ref[0, :, span], span


def one_hot(cell):
    row = lax.broadcasted_iota(jnp.int32, (CX * CY, TILE), 0)
    return jnp.where(row == (cell >> 7), 1.0, 0.0).astype(BF16)


def spread_kernel(
    par_ref, count_ref, cell_hbm, frac_hbm, charge_hbm,
    grid_ref, mc_ref, s1_ref, s2_ref, t1_ref, t2_ref, live_ref,
    cell_ref, frac_ref, charge_ref, planes_ref, acc_ref, sems,
):
    copies = [
        pltpu.make_async_copy(src, dst, sems.at[k])
        for k, (src, dst) in enumerate(
            (
                (cell_hbm, cell_ref),
                (frac_hbm, frac_ref),
                (charge_hbm, charge_ref),
            )
        )
    ]
    for copy in copies:
        copy.start()
    acc_ref[...] = jnp.zeros_like(acc_ref)
    grid_ref[...] = jnp.zeros_like(grid_ref)
    planes_ref[0:144] = plane_tents(2)
    planes_ref[144:288] = plane_tents(4)
    for copy in copies:
        copy.wait()
    slot = lax.broadcasted_iota(jnp.int32, (1, ATOMS), 1)
    live_ref[0] = jnp.where(slot < count_ref[0, 0], charge_ref[0], 0.0)

    def step(t, carry):
        cell, f, charge, _ = rows_of(cell_ref, frac_ref, live_ref, t)
        hot = one_hot(cell)
        z = cell & (NZ - 1)
        plane = lax.broadcasted_iota(jnp.int32, (NZ, TILE), 0)
        at_low = plane == z
        at_high = plane == ((z + 1) & (NZ - 1))
        wx = [1.0 - f[0], f[0]]
        wy = [1.0 - f[1], f[1]]
        wz = [1.0 - f[2], f[2]]
        highs = []
        lows = []
        for ab in range(4):
            flat = charge * wx[ab >> 1] * wy[ab & 1]
            weights = [flat * wz[e] for e in range(2)]
            tops = [w.astype(BF16).astype(F32) for w in weights]
            for group, (w0, w1) in (
                (highs, tops),
                (lows, [w - t for w, t in zip(weights, tops)]),
            ):
                group.append(
                    jnp.where(at_low, w0, jnp.where(at_high, w1, 0.0)).astype(BF16)
                )
        dims = (((1,), (1,)), ((), ()))
        acc_ref[...] += sum(
            lax.dot_general(
                hot, jnp.concatenate(group, axis=0), dims, preferred_element_type=F32
            )
            for group in (highs, lows)
        )
        return carry

    lax.fori_loop(0, ATOMS // TILE, step, 0)
    for ab in range(4):
        a, b = ab >> 1, ab & 1
        for x in range(CX):
            grid_ref[x + a, b : b + CY, :] += acc_ref[
                x * CY : (x + 1) * CY, ab * NZ : (ab + 1) * NZ
            ]
    grid = grid_ref[...].reshape((CX + 1) * 32, NZ)
    small = dot_exact(planes_ref[...], grid)
    mc = dot_right(small[:144], depth_tents(2, 0)) + dot_right(small[144:], depth_tents(4, 64))
    mc_ref[...] = mc.reshape(9, 16, NZ)

    even = par_ref[0] == 0
    even2 = par_ref[1] == 0
    is_coarse = coarse_lanes((5, 16, NZ))

    def put_low(ref):
        ref[:, :32, :] = grid_ref[0:5]
        ref[:, 32:, :] = mc_ref[0:5]

    def put_high(ref):
        ref[:, :32, :] = grid_ref[12:17]
        ref[:, 32:, :] = jnp.where(is_coarse, mc_ref[0:5], mc_ref[4:9])

    @pl.when(even)
    def _():
        put_high(s1_ref)
        put_low(s2_ref)

    @pl.when(jnp.logical_not(even))
    def _():
        put_low(s1_ref)
        put_high(s2_ref)

    @pl.when(even2)
    def _():
        t1_ref[...] = mc_ref[4]
        t2_ref[...] = mc_ref[0]

    @pl.when(jnp.logical_not(even2))
    def _():
        t1_ref[...] = mc_ref[0]
        t2_ref[...] = mc_ref[4]


def taps_kernel(
    fine_hbm, middle_hbm, coarse_hbm, packed_hbm, live_ref, h_ref,
    fine_ref, middle_ref, coarse_ref, packed_ref, sems,
):
    first = PLACES["spread_high"][0]
    pairs = (
        (fine_hbm, fine_ref),
        (middle_hbm, middle_ref),
        (coarse_hbm, coarse_ref),
        (packed_hbm.at[first : PACKED.shape[0]], packed_ref),
    )
    copies = [pltpu.make_async_copy(*pair, sems.at[k]) for k, pair in enumerate(pairs)]
    for copy in copies:
        copy.start()
    for copy in copies:
        copy.wait()
    levels = [
        (ref, whole(packed_ref, name, first)[:KERNEL])
        for ref, name in ((fine_ref, "tap128"), (middle_ref, "tap64"), (coarse_ref, "tap32"))
    ]
    spread = whole(packed_ref, "spread", first)
    for a in range(KERNEL):
        along_z = sum(dot(ref[a], tap) for ref, tap in levels)
        both = dot(spread, along_z)
        h_ref[a, :, :NZ] = both[:40, :NZ] - both[40:, NZ:]
        h_ref[a, :, NZ:] = both[:40, NZ:] + both[40:, :NZ]


def merge_kernel(
    par_ref, shat_ref, mc_ref, r1_ref, r2_ref, rt1_ref, rt2_ref, h_ref,
    e_ref, g_ref, s1_ref, s2_ref,
):
    e_ref[0:4] = jnp.zeros((4, 32, NZ), F32)
    e_ref[21:25] = jnp.zeros((4, 32, NZ), F32)
    e_ref[4:21] = shat_ref[...]
    g_ref[0:4] = jnp.zeros((4, 16, NZ), F32)
    g_ref[13:17] = jnp.zeros((4, 16, NZ), F32)
    g_ref[4:13] = mc_ref[...]
    is_coarse = coarse_lanes((5, 16, NZ))

    def merge(low_ref, high_ref):
        e_ref[0:5] += low_ref[:, :32, :]
        e_ref[20:25] += high_ref[:, :32, :]
        g_ref[0:5] += low_ref[:, 32:, :]
        high = high_ref[:, 32:, :]
        g_ref[12:17] += jnp.where(is_coarse, 0.0, high)
        g_ref[8:13] += jnp.where(is_coarse, high, 0.0)

    def merge2(low_ref, high_ref):
        g_ref[0] += jnp.where(is_coarse[0], low_ref[...], 0.0)
        g_ref[12] += jnp.where(is_coarse[0], high_ref[...], 0.0)

    even = par_ref[0] == 0
    even2 = par_ref[1] == 0

    @pl.when(even)
    def _():
        merge(r2_ref, r1_ref)

    @pl.when(jnp.logical_not(even))
    def _():
        merge(r1_ref, r2_ref)

    @pl.when(even2)
    def _():
        merge2(rt2_ref, rt1_ref)

    @pl.when(jnp.logical_not(even2))
    def _():
        merge2(rt1_ref, rt2_ref)

    def put_low(ref):
        ref[0:25] = e_ref[:, 0:8, :]
        ref[25:42] = g_ref[:, 0:8, :]

    def put_high(ref):
        ref[0:25, 0:5, :] = e_ref[:, 20:25, :]
        ref[0:25, 5:8, :] = jnp.zeros((25, 3, NZ), F32)
        ref[25:42] = jnp.where(
            coarse_lanes((17, 8, NZ)), g_ref[:, 2:10, :], g_ref[:, 8:16, :]
        )

    y_even = par_ref[2] == 0

    @pl.when(y_even)
    def _():
        put_high(s1_ref)
        put_low(s2_ref)

    @pl.when(jnp.logical_not(y_even))
    def _():
        put_low(s1_ref)
        put_high(s2_ref)


def finish_kernel(
    par_ref, e_ref, g_ref, r1_ref, r2_ref, h_ref, cell_ref, frac_ref, charge_ref, packed_ref,
    pot_ref, force_ref,
    ee_ref, gg_ref, z_ref, v_ref, o_ref, w_ref, full_ref, turned_ref,
):
    for ref, wide, src in ((ee_ref, 32, e_ref), (gg_ref, 16, g_ref)):
        ref[:, 0:4, :] = jnp.zeros((ref.shape[0], 4, NZ), F32)
        ref[:, 4 + wide :, :] = jnp.zeros((ref.shape[0], 4, NZ), F32)
        ref[:, 4 : 4 + wide, :] = src[...]
    is_coarse = coarse_lanes((17, 5, NZ))

    def merge(low_ref, high_ref):
        ee_ref[:, 0:5, :] += low_ref[0:25, 0:5, :]
        ee_ref[:, 28:33, :] += high_ref[0:25, 0:5, :]
        gg_ref[:, 0:5, :] += low_ref[25:42, 0:5, :]
        high = high_ref[25:42, 0:5, :]
        gg_ref[:, 16:21, :] += jnp.where(is_coarse, 0.0, high)
        gg_ref[:, 10:15, :] += jnp.where(is_coarse, high, 0.0)

    y_even = par_ref[2] == 0

    @pl.when(y_even)
    def _():
        merge(r2_ref, r1_ref)

    @pl.when(jnp.logical_not(y_even))
    def _():
        merge(r1_ref, r2_ref)

    z_ref[...] = dot3(split(ee_ref[...].reshape(1000, NZ)), table(packed_ref, "forward")).reshape(25, 40, 256)
    z_ref[0:17, 0:24, :] += dot3(split(gg_ref[...].reshape(408, NZ)), table(packed_ref, "small")).reshape(
        17, 24, 256
    )
    for group in range(5):
        rows = slice(5 * group, 5 * group + 5)
        both = dot3(table(packed_ref, "line"), split(z_ref[rows].reshape(200, 256)))
        v_ref[rows, :, :NZ] = (both[:200, :NZ] - both[200:, NZ:]).reshape(5, 40, NZ)
        v_ref[rows, :, NZ:] = (both[:200, NZ:] + both[200:, :NZ]).reshape(5, 40, NZ)

    o_ref[CX + 1] = jnp.zeros((40, 256), F32)

    def across(t, carry):
        rows = pl.ds(pl.multiple_of(t * 8, 8), 8)
        for part in range(2):
            acc = [jnp.zeros((8, NZ), F32) for _ in range(CX + 1)]
            for xin in range(CX + KERNEL):
                real = v_ref[xin, rows, :NZ]
                imag = v_ref[xin, rows, NZ:]
                for a in range(KERNEL):
                    x = xin - a
                    if 0 <= x <= CX:
                        h_real = h_ref[a, rows, :NZ]
                        h_imag = h_ref[a, rows, NZ:]
                        if part == 0:
                            acc[x] = acc[x] + real * h_real - imag * h_imag
                        else:
                            acc[x] = acc[x] + real * h_imag + imag * h_real
            for x in range(CX + 1):
                o_ref[x, rows, part * NZ : (part + 1) * NZ] = acc[x]
        return carry

    lax.fori_loop(0, 5, across, 0)
    for group in range(3):
        rows = slice(6 * group, 6 * group + 6)
        both = dot3(table(packed_ref, "back"), split(o_ref[rows].reshape(240, 256)))
        w_ref[rows, :, :NZ] = (both[:192, :NZ] - both[192:, NZ:]).reshape(6, 32, NZ)
        w_ref[rows, :, NZ:] = (both[:192, NZ:] + both[192:, :NZ]).reshape(6, 32, NZ)
    both = dot3(split(w_ref[0:9, 0:16, :].reshape(144, 256)), table(packed_ref, "levels"))
    full = dot3(split(w_ref[0 : CX + 1].reshape((CX + 1) * 32, 256)), table(packed_ref, "inverse"))
    for k, name in enumerate(("plane2", "plane4")):
        full += dot_exact(table(packed_ref, name), both[:, k * NZ : (k + 1) * NZ])
    full_ref[...] = full.reshape(CX + 1, 32, NZ)
    pot_ref[...] = full_ref[0:CX, 0:CY, :]
    for ab in range(4):
        a, b = ab >> 1, ab & 1
        part = full_ref[a : a + CX, b : b + CY, :].reshape(CX * CY, NZ).T
        high, low = split(part)
        turned_ref[ab * NZ : (ab + 1) * NZ, : CX * CY] = high
        turned_ref[ab * NZ : (ab + 1) * NZ, CX * CY :] = low

    def step(t, carry):
        cell, f, charge, span = rows_of(cell_ref, frac_ref, charge_ref, t)
        hot = one_hot(cell)
        hot = jnp.concatenate([hot, hot], axis=0)
        z = cell & (NZ - 1)
        plane = lax.broadcasted_iota(jnp.int32, (NZ, TILE), 0)
        at_low = plane == z
        at_high = plane == ((z + 1) & (NZ - 1))
        corner = []
        for ab in range(4):
            rows = slice(ab * NZ, (ab + 1) * NZ)
            found = jnp.dot(turned_ref[rows, :], hot, preferred_element_type=F32)
            corner.append(
                [
                    jnp.sum(jnp.where(mask, found, 0.0), axis=0, keepdims=True)
                    for mask in (at_low, at_high)
                ]
            )
        wx = [1.0 - f[0], f[0]]
        wy = [1.0 - f[1], f[1]]
        wz = [1.0 - f[2], f[2]]
        sign = [-1.0, 1.0]
        sums = [0.0, 0.0, 0.0]
        for a in range(2):
            for b in range(2):
                for e in range(2):
                    v = corner[2 * a + b][e]
                    sums[0] = sums[0] + sign[a] * wy[b] * wz[e] * v
                    sums[1] = sums[1] + wx[a] * sign[b] * wz[e] * v
                    sums[2] = sums[2] + wx[a] * wy[b] * sign[e] * v
        for k in range(3):
            force_ref[k, 0, :, span] = -charge * sums[k]
        return carry

    lax.fori_loop(0, ATOMS // TILE, step, 0)


def call(kernel, outs, args, spaces, scratch=()):
    return pl.pallas_call(
        kernel,
        out_shape=[jax.ShapeDtypeStruct(shape, F32) for shape in outs],
        in_specs=[pl.BlockSpec(memory_space=space) for space in spaces],
        out_specs=[pl.BlockSpec(memory_space=pltpu.VMEM) for _ in outs],
        scratch_shapes=list(scratch),
        compiler_params=pltpu.CompilerParams(vmem_limit_bytes=VMEM_LIMIT),
    )(*args)


def in_hbm(*values):
    return [pltpu.with_memory_space_constraint(value, pltpu.HBM) for value in values]


def swap(value, axis, first, gap):
    pairs = []
    for i in range(16):
        partner = ((((i - first) % 16) ^ gap) + first) % 16
        pairs.append((i, partner))
    return lax.ppermute(value, axis, pairs)


def per_device(cell, frac, charge, count, fine, middle, coarse):
    packed = jnp.asarray(PACKED)
    ix, iy = lax.axis_index("gx"), lax.axis_index("gy")
    par = jnp.stack([ix & 1, (ix >> 1) & 1, iy & 1]).astype(jnp.int32)
    shat, mc, s1, s2, t1, t2, live = call(
        spread_kernel,
        [(17, 32, NZ), (9, 16, NZ), (5, 48, NZ), (5, 48, NZ), (16, NZ), (16, NZ), (1, 1, ATOMS)],
        (par, count, *in_hbm(cell, frac, charge)),
        [pltpu.SMEM] * 2 + [pltpu.HBM] * 3,
        [
            pltpu.VMEM((1, 1, ATOMS), jnp.int32),
            pltpu.VMEM((3, 1, 1, ATOMS), F32),
            pltpu.VMEM((1, 1, ATOMS), F32),
            pltpu.VMEM((288, (CX + 1) * 32), BF16),
            pltpu.VMEM((CX * CY, 4 * NZ), F32),
            pltpu.SemaphoreType.DMA((3,)),
        ],
    )
    r1 = swap(s1, "gx", 0, 1)
    r2 = swap(s2, "gx", 1, 1)
    rt1 = swap(t1, "gx", 0, 2)
    rt2 = swap(t2, "gx", 2, 2)
    (h,) = call(
        taps_kernel,
        [(KERNEL, 40, 256)],
        (*in_hbm(fine, middle, coarse, packed), live),
        [pltpu.HBM] * 4 + [pl.ANY],
        [
            pltpu.VMEM((KERNEL, KERNEL, KERNEL), F32),
            pltpu.VMEM((KERNEL, KERNEL, KERNEL), F32),
            pltpu.VMEM((KERNEL, KERNEL, KERNEL), F32),
            pltpu.VMEM((PACKED.shape[0] - PLACES["spread_high"][0], 256), BF16),
            pltpu.SemaphoreType.DMA((4,)),
        ],
    )
    e, g, y1, y2 = call(
        merge_kernel,
        [(25, 32, NZ), (17, 16, NZ), (42, 8, NZ), (42, 8, NZ)],
        (par, shat, mc, r1, r2, rt1, rt2, h),
        [pltpu.SMEM] + [pltpu.VMEM] * 6 + [pl.ANY],
    )
    q1 = swap(y1, "gy", 0, 1)
    q2 = swap(y2, "gy", 1, 1)
    pot, force = call(
        finish_kernel,
        [(CX, CY, NZ), (3, 1, 1, ATOMS)],
        (par, e, g, q1, q2, h, cell, frac, live, packed),
        [pltpu.SMEM] + [pltpu.VMEM] * 9,
        [
            pltpu.VMEM((25, 40, NZ), F32),
            pltpu.VMEM((17, 24, NZ), F32),
            pltpu.VMEM((25, 40, 256), F32),
            pltpu.VMEM((25, 40, 256), F32),
            pltpu.VMEM((18, 40, 256), F32),
            pltpu.VMEM((18, 32, 256), F32),
            pltpu.VMEM((CX + 1, 32, NZ), F32),
            pltpu.VMEM((4 * NZ, 2 * CX * CY), BF16),
        ],
    )
    return pot, force


def solution(mesh):
    return jax.shard_map(
        per_device,
        mesh=mesh,
        in_specs=(
            P("gx", "gy", None),
            P(None, "gx", "gy", None),
            P("gx", "gy", None),
            P("gx", "gy"),
            P(),
            P(),
            P(),
        ),
        out_specs=(P("gx", "gy", None), P(None, "gx", "gy", None)),
        check_vma=False,
    )
```

```python
import functools

import jax
import jax.numpy as jnp
import numpy as np
from jax import lax
from jax.experimental import pallas as pl
from jax.experimental.pallas import tpu as pltpu
from jax.sharding import PartitionSpec as P

CX = 16
CY = 24
NZ = 128
ATOMS = 4096
KERNEL = 9
TILE = 1024
HIGHEST = lax.Precision.HIGHEST
F32 = jnp.float32
BF16 = jnp.bfloat16
VMEM_LIMIT = 48 * 1024 * 1024


LINE = CY + KERNEL
FIRST = {128: 0, 64: 65, 32: 98}


def forward_table(n):
    z, k = np.arange(n)[:, None], np.arange(n // 2 + 1)[None, :]
    turn = np.exp(-2j * np.pi * k * z / n)
    return placed(turn, n)


def placed(turn, n):
    out = np.zeros((turn.shape[0], 256))
    first, count = FIRST[n], n // 2 + 1
    out[:, first : first + count] = turn.real
    out[:, 128 + first : 128 + first + count] = turn.imag
    return out


def inverse_table(n):
    z, k = np.arange(n)[:, None], np.arange(n // 2 + 1)[None, :]
    weight = np.where((k == 0) | (k == n // 2), 1.0, 2.0) / n
    return placed(weight * np.exp(-2j * np.pi * k * z / n), n).T


def tap_tables(n):
    c, k = np.arange(KERNEL)[:, None] - KERNEL // 2, np.arange(n // 2 + 1)[None, :]
    return placed(np.exp(2j * np.pi * k * c / n), n)


def line_tables():
    k = np.arange(LINE)
    forward = np.zeros((40, 40), complex)
    forward[:LINE, :LINE] = np.exp(-2j * np.pi * np.outer(k, k) / LINE)
    back = np.zeros((32, 40), complex)
    back[: CY + 1, :LINE] = np.exp(2j * np.pi * np.outer(np.arange(CY + 1), k) / LINE) / LINE
    spread = np.zeros((40, KERNEL), complex)
    spread[:LINE] = np.exp(2j * np.pi * np.outer(k, np.arange(KERNEL)) / LINE)

    def both(table, copies):
        return np.concatenate(
            [np.kron(np.eye(copies), table.real), np.kron(np.eye(copies), table.imag)], axis=0
        )

    return both(forward, 5), both(back, 6), both(spread, 1)


def restrict_z(n):
    out = np.zeros((n, n // 2))
    for i in range(n // 2):
        out[(2 * i - 1) % n, i] += 0.5
        out[2 * i, i] += 1.0
        out[(2 * i + 1) % n, i] += 0.5
    return out


def prolong_z(n):
    return restrict_z(2 * n).T


def tents(fine, step, coarse):
    far = np.abs(np.arange(fine)[None, :] - step * np.arange(coarse)[:, None])
    return np.maximum(0.0, 1.0 - far / step)


def plane_table(step):
    cx, cy = CX // step + 1, CY // step + 1
    along_x = tents(CX + 1, step, cx)
    along_y = tents(CY + 1, step, cy)
    out = np.zeros((9, 16, CX + 1, 32))
    out[:cx, :cy, :, : CY + 1] = along_x[:, None, :, None] * along_y[None, :, None, :]
    return out.reshape(144, (CX + 1) * 32)


def halves(table):
    table = np.asarray(table, np.float32)
    high = table.astype(BF16)
    return np.stack([high, (table - high.astype(np.float32)).astype(BF16)])


def tables():
    small = np.zeros((128, 256))
    small[:64] = forward_table(64)
    small[64:96] = forward_table(32)
    line, back, spread = line_tables()
    inverse = np.concatenate(
        [
            inverse_table(64) @ prolong_z(64),
            inverse_table(32) @ prolong_z(32) @ prolong_z(64),
        ],
        axis=1,
    )
    parts = {
        "plane2": np.asarray(plane_table(2).T, BF16),
        "plane4": np.asarray(plane_table(4).T, BF16),
    }
    for name, table in (
        ("forward", forward_table(128)),
        ("small", small),
        ("line", line),
        ("back", back),
        ("inverse", inverse_table(128)),
        ("levels", inverse),
        ("spread", spread),
        ("tap128", tap_tables(128)),
        ("tap64", tap_tables(64)),
        ("tap32", tap_tables(32)),
    ):
        parts[name + "_high"], parts[name + "_low"] = halves(table)
    places = {}
    blocks = []
    start = 0
    for name, part in parts.items():
        rows, cols = part.shape
        whole = -(-rows // 16) * 16
        places[name] = (start, whole, cols)
        blocks.append(np.pad(part, ((0, whole - rows), (0, 256 - cols))))
        start += whole
    return np.concatenate(blocks, axis=0), places


PACKED, PLACES = tables()


def table(ref, name, first=0):
    if name + "_high" in PLACES:
        return table(ref, name + "_high", first), table(ref, name + "_low", first)
    start, rows, cols = PLACES[name]
    return ref[start - first : start - first + rows, :cols]


def whole(ref, name, first):
    high, low = table(ref, name, first)
    return high.astype(F32) + low.astype(F32)


def dot(a, b):
    return jnp.dot(a, b, precision=HIGHEST, preferred_element_type=F32)


def dot_exact(table, value):
    high, low = split(value)
    return jnp.dot(table, high, preferred_element_type=F32) + jnp.dot(
        table, low, preferred_element_type=F32
    )


def split(value):
    high = value.astype(BF16)
    return high, (value - high.astype(F32)).astype(BF16)


def dot3(a, b):
    total = jnp.dot(a[0], b[0], preferred_element_type=F32)
    total += jnp.dot(a[0], b[1], preferred_element_type=F32)
    return total + jnp.dot(a[1], b[0], preferred_element_type=F32)


def tent(far, step):
    return jnp.maximum(step - jnp.abs(far), 0)


def plane_tents(step):
    row = lax.broadcasted_iota(jnp.int32, (144, (CX + 1) * 32), 0)
    col = lax.broadcasted_iota(jnp.int32, (144, (CX + 1) * 32), 1)
    along_x = tent((col >> 5) - step * (row >> 4), step)
    along_y = tent((col & 31) - step * (row & 15), step)
    return ((along_x * along_y).astype(F32) * (1.0 / step**2)).astype(BF16)


def depth_tents(step, first):
    row = lax.broadcasted_iota(jnp.int32, (NZ, NZ), 0)
    col = lax.broadcasted_iota(jnp.int32, (NZ, NZ), 1) - first
    far = (row - step * col) & (NZ - 1)
    weight = tent(far, step) + tent(NZ - far, step)
    weight = jnp.where((col >= 0) & (col < NZ // step), weight, 0)
    return (weight.astype(F32) * (1.0 / step)).astype(BF16)


def dot_right(value, table):
    high, low = split(value)
    return jnp.dot(high, table, preferred_element_type=F32) + jnp.dot(
        low, table, preferred_element_type=F32
    )


def coarse_lanes(shape):
    return lax.broadcasted_iota(jnp.int32, shape, len(shape) - 1) >= 64


def rows_of(cell_ref, frac_ref, charge_ref, t):
    span = pl.ds(t * TILE, TILE)
    cell = cell_ref[0, :, span]
    f = [frac_ref[k, 0, :, span] for k in range(3)]
    return cell, f, charge_ref[0, :, span], span


def one_hot(cell):
    row = lax.broadcasted_iota(jnp.int32, (CX * CY, TILE), 0)
    return jnp.where(row == (cell >> 7), 1.0, 0.0).astype(BF16)


def spread_kernel(
    par_ref, count_ref, cell_hbm, frac_hbm, charge_hbm,
    grid_ref, mc_ref, s1_ref, s2_ref, t1_ref, t2_ref, live_ref,
    cell_ref, frac_ref, charge_ref, planes_ref, acc_ref, sems,
):
    copies = [
        pltpu.make_async_copy(src, dst, sems.at[k])
        for k, (src, dst) in enumerate(
            (
                (cell_hbm, cell_ref),
                (frac_hbm, frac_ref),
                (charge_hbm, charge_ref),
            )
        )
    ]
    for copy in copies:
        copy.start()
    acc_ref[...] = jnp.zeros_like(acc_ref)
    grid_ref[...] = jnp.zeros_like(grid_ref)
    planes_ref[0:144] = plane_tents(2)
    planes_ref[144:288] = plane_tents(4)
    for copy in copies:
        copy.wait()
    slot = lax.broadcasted_iota(jnp.int32, (1, ATOMS), 1)
    live_ref[0] = jnp.where(slot < count_ref[0, 0], charge_ref[0], 0.0)

    def step(t, carry):
        cell, f, charge, _ = rows_of(cell_ref, frac_ref, live_ref, t)
        hot = one_hot(cell)
        z = cell & (NZ - 1)
        plane = lax.broadcasted_iota(jnp.int32, (NZ, TILE), 0)
        at_low = plane == z
        at_high = plane == ((z + 1) & (NZ - 1))
        wx = [1.0 - f[0], f[0]]
        wy = [1.0 - f[1], f[1]]
        wz = [1.0 - f[2], f[2]]
        low_hot = jnp.where(at_low, 1.0, 0.0).astype(BF16)
        high_hot = jnp.where(at_high, 1.0, 0.0).astype(BF16)
        highs = []
        lows = []
        for ab in range(4):
            flat = charge * wx[ab >> 1] * wy[ab & 1]
            weights = [flat * wz[e] for e in range(2)]
            tops = [w.astype(BF16).astype(F32) for w in weights]
            for group, (w0, w1) in (
                (highs, tops),
                (lows, [w - t for w, t in zip(weights, tops)]),
            ):
                group.append(low_hot * w0.astype(BF16) + high_hot * w1.astype(BF16))
        dims = (((1,), (1,)), ((), ()))
        acc_ref[...] += sum(
            lax.dot_general(
                hot, jnp.concatenate(group, axis=0), dims, preferred_element_type=F32
            )
            for group in (highs, lows)
        )
        return carry

    lax.fori_loop(0, ATOMS // TILE, step, 0, unroll=True)
    for ab in range(4):
        a, b = ab >> 1, ab & 1
        for x in range(CX):
            grid_ref[x + a, b : b + CY, :] += acc_ref[
                x * CY : (x + 1) * CY, ab * NZ : (ab + 1) * NZ
            ]
    grid = grid_ref[...].reshape((CX + 1) * 32, NZ)
    small = dot_exact(planes_ref[...], grid)
    mc = dot_right(small[:144], depth_tents(2, 0)) + dot_right(small[144:], depth_tents(4, 64))
    mc_ref[...] = mc.reshape(9, 16, NZ)

    even = par_ref[0] == 0
    even2 = par_ref[1] == 0
    is_coarse = coarse_lanes((5, 16, NZ))

    def put_low(ref):
        ref[:, :32, :] = grid_ref[0:5]
        ref[:, 32:, :] = mc_ref[0:5]

    def put_high(ref):
        ref[:, :32, :] = grid_ref[12:17]
        ref[:, 32:, :] = jnp.where(is_coarse, mc_ref[0:5], mc_ref[4:9])

    @pl.when(even)
    def _():
        put_high(s1_ref)
        put_low(s2_ref)

    @pl.when(jnp.logical_not(even))
    def _():
        put_low(s1_ref)
        put_high(s2_ref)

    @pl.when(even2)
    def _():
        t1_ref[...] = mc_ref[4]
        t2_ref[...] = mc_ref[0]

    @pl.when(jnp.logical_not(even2))
    def _():
        t1_ref[...] = mc_ref[0]
        t2_ref[...] = mc_ref[4]


def taps_kernel(
    fine_hbm, middle_hbm, coarse_hbm, packed_hbm, live_ref, h_ref,
    fine_ref, middle_ref, coarse_ref, packed_ref, sems,
):
    first = PLACES["spread_high"][0]
    pairs = (
        (fine_hbm, fine_ref),
        (middle_hbm, middle_ref),
        (coarse_hbm, coarse_ref),
        (packed_hbm.at[first : PACKED.shape[0]], packed_ref),
    )
    copies = [pltpu.make_async_copy(*pair, sems.at[k]) for k, pair in enumerate(pairs)]
    for copy in copies:
        copy.start()
    for copy in copies:
        copy.wait()
    levels = [
        (ref, whole(packed_ref, name, first)[:KERNEL])
        for ref, name in ((fine_ref, "tap128"), (middle_ref, "tap64"), (coarse_ref, "tap32"))
    ]
    spread = whole(packed_ref, "spread", first)
    for a in range(KERNEL):
        along_z = sum(dot(ref[a], tap) for ref, tap in levels)
        both = dot(spread, along_z)
        h_ref[a, :, :NZ] = both[:40, :NZ] - both[40:, NZ:]
        h_ref[a, :, NZ:] = both[:40, NZ:] + both[40:, :NZ]


def merge_kernel(
    par_ref, shat_ref, mc_ref, r1_ref, r2_ref, rt1_ref, rt2_ref, h_ref,
    e_ref, g_ref, s1_ref, s2_ref,
):
    e_ref[0:4] = jnp.zeros((4, 32, NZ), F32)
    e_ref[21:25] = jnp.zeros((4, 32, NZ), F32)
    e_ref[4:21] = shat_ref[...]
    g_ref[0:4] = jnp.zeros((4, 16, NZ), F32)
    g_ref[13:17] = jnp.zeros((4, 16, NZ), F32)
    g_ref[4:13] = mc_ref[...]
    is_coarse = coarse_lanes((5, 16, NZ))

    def merge(low_ref, high_ref):
        e_ref[0:5] += low_ref[:, :32, :]
        e_ref[20:25] += high_ref[:, :32, :]
        g_ref[0:5] += low_ref[:, 32:, :]
        high = high_ref[:, 32:, :]
        g_ref[12:17] += jnp.where(is_coarse, 0.0, high)
        g_ref[8:13] += jnp.where(is_coarse, high, 0.0)

    def merge2(low_ref, high_ref):
        g_ref[0] += jnp.where(is_coarse[0], low_ref[...], 0.0)
        g_ref[12] += jnp.where(is_coarse[0], high_ref[...], 0.0)

    even = par_ref[0] == 0
    even2 = par_ref[1] == 0

    @pl.when(even)
    def _():
        merge(r2_ref, r1_ref)

    @pl.when(jnp.logical_not(even))
    def _():
        merge(r1_ref, r2_ref)

    @pl.when(even2)
    def _():
        merge2(rt2_ref, rt1_ref)

    @pl.when(jnp.logical_not(even2))
    def _():
        merge2(rt1_ref, rt2_ref)

    def put_low(ref):
        ref[0:25] = e_ref[:, 0:8, :]
        ref[25:42] = g_ref[:, 0:8, :]

    def put_high(ref):
        ref[0:25, 0:5, :] = e_ref[:, 20:25, :]
        ref[0:25, 5:8, :] = jnp.zeros((25, 3, NZ), F32)
        ref[25:42] = jnp.where(
            coarse_lanes((17, 8, NZ)), g_ref[:, 2:10, :], g_ref[:, 8:16, :]
        )

    y_even = par_ref[2] == 0

    @pl.when(y_even)
    def _():
        put_high(s1_ref)
        put_low(s2_ref)

    @pl.when(jnp.logical_not(y_even))
    def _():
        put_low(s1_ref)
        put_high(s2_ref)


def finish_kernel(
    par_ref, e_ref, g_ref, r1_ref, r2_ref, h_ref, cell_ref, frac_ref, charge_ref, packed_ref,
    pot_ref, force_ref,
    ee_ref, gg_ref, z_ref, v_ref, o_ref, w_ref, full_ref, turned_ref,
):
    for ref, wide, src in ((ee_ref, 32, e_ref), (gg_ref, 16, g_ref)):
        ref[:, 0:4, :] = jnp.zeros((ref.shape[0], 4, NZ), F32)
        ref[:, 4 + wide :, :] = jnp.zeros((ref.shape[0], 4, NZ), F32)
        ref[:, 4 : 4 + wide, :] = src[...]
    is_coarse = coarse_lanes((17, 5, NZ))

    def merge(low_ref, high_ref):
        ee_ref[:, 0:5, :] += low_ref[0:25, 0:5, :]
        ee_ref[:, 28:33, :] += high_ref[0:25, 0:5, :]
        gg_ref[:, 0:5, :] += low_ref[25:42, 0:5, :]
        high = high_ref[25:42, 0:5, :]
        gg_ref[:, 16:21, :] += jnp.where(is_coarse, 0.0, high)
        gg_ref[:, 10:15, :] += jnp.where(is_coarse, high, 0.0)

    y_even = par_ref[2] == 0

    @pl.when(y_even)
    def _():
        merge(r2_ref, r1_ref)

    @pl.when(jnp.logical_not(y_even))
    def _():
        merge(r1_ref, r2_ref)

    z_ref[...] = dot3(split(ee_ref[...].reshape(1000, NZ)), table(packed_ref, "forward")).reshape(25, 40, 256)
    z_ref[0:17, 0:24, :] += dot3(split(gg_ref[...].reshape(408, NZ)), table(packed_ref, "small")).reshape(
        17, 24, 256
    )
    for group in range(5):
        rows = slice(5 * group, 5 * group + 5)
        both = dot3(table(packed_ref, "line"), split(z_ref[rows].reshape(200, 256)))
        v_ref[rows, :, :NZ] = (both[:200, :NZ] - both[200:, NZ:]).reshape(5, 40, NZ)
        v_ref[rows, :, NZ:] = (both[:200, NZ:] + both[200:, :NZ]).reshape(5, 40, NZ)

    o_ref[CX + 1] = jnp.zeros((40, 256), F32)

    def across(t, carry):
        rows = pl.ds(pl.multiple_of(t * 8, 8), 8)
        for part in range(2):
            acc = [jnp.zeros((8, NZ), F32) for _ in range(CX + 1)]
            for xin in range(CX + KERNEL):
                real = v_ref[xin, rows, :NZ]
                imag = v_ref[xin, rows, NZ:]
                for a in range(KERNEL):
                    x = xin - a
                    if 0 <= x <= CX:
                        h_real = h_ref[a, rows, :NZ]
                        h_imag = h_ref[a, rows, NZ:]
                        if part == 0:
                            acc[x] = acc[x] + real * h_real - imag * h_imag
                        else:
                            acc[x] = acc[x] + real * h_imag + imag * h_real
            for x in range(CX + 1):
                o_ref[x, rows, part * NZ : (part + 1) * NZ] = acc[x]
        return carry

    lax.fori_loop(0, 5, across, 0)
    for group in range(3):
        rows = slice(6 * group, 6 * group + 6)
        both = dot3(table(packed_ref, "back"), split(o_ref[rows].reshape(240, 256)))
        w_ref[rows, :, :NZ] = (both[:192, :NZ] - both[192:, NZ:]).reshape(6, 32, NZ)
        w_ref[rows, :, NZ:] = (both[:192, NZ:] + both[192:, :NZ]).reshape(6, 32, NZ)
    both = dot3(split(w_ref[0:9, 0:16, :].reshape(144, 256)), table(packed_ref, "levels"))
    full = dot3(split(w_ref[0 : CX + 1].reshape((CX + 1) * 32, 256)), table(packed_ref, "inverse"))
    for k, name in enumerate(("plane2", "plane4")):
        full += dot_exact(table(packed_ref, name), both[:, k * NZ : (k + 1) * NZ])
    full_ref[...] = full.reshape(CX + 1, 32, NZ)
    pot_ref[...] = full_ref[0:CX, 0:CY, :]
    for ab in range(4):
        a, b = ab >> 1, ab & 1
        part = full_ref[a : a + CX, b : b + CY, :].reshape(CX * CY, NZ).T
        high, low = split(part)
        turned_ref[ab * NZ : (ab + 1) * NZ, : CX * CY] = high
        turned_ref[ab * NZ : (ab + 1) * NZ, CX * CY :] = low

    def step(t, carry):
        cell, f, charge, span = rows_of(cell_ref, frac_ref, charge_ref, t)
        hot = one_hot(cell)
        hot = jnp.concatenate([hot, hot], axis=0)
        z = cell & (NZ - 1)
        plane = lax.broadcasted_iota(jnp.int32, (NZ, TILE), 0)
        at_low = plane == z
        at_high = plane == ((z + 1) & (NZ - 1))
        corner = []
        for ab in range(4):
            rows = slice(ab * NZ, (ab + 1) * NZ)
            found = jnp.dot(turned_ref[rows, :], hot, preferred_element_type=F32)
            corner.append(
                [
                    jnp.sum(jnp.where(mask, found, 0.0), axis=0, keepdims=True)
                    for mask in (at_low, at_high)
                ]
            )
        wx = [1.0 - f[0], f[0]]
        wy = [1.0 - f[1], f[1]]
        wz = [1.0 - f[2], f[2]]
        sign = [-1.0, 1.0]
        sums = [0.0, 0.0, 0.0]
        for a in range(2):
            for b in range(2):
                for e in range(2):
                    v = corner[2 * a + b][e]
                    sums[0] = sums[0] + sign[a] * wy[b] * wz[e] * v
                    sums[1] = sums[1] + wx[a] * sign[b] * wz[e] * v
                    sums[2] = sums[2] + wx[a] * wy[b] * sign[e] * v
        for k in range(3):
            force_ref[k, 0, :, span] = -charge * sums[k]
        return carry

    lax.fori_loop(0, ATOMS // TILE, step, 0)


def call(kernel, outs, args, spaces, scratch=()):
    return pl.pallas_call(
        kernel,
        out_shape=[jax.ShapeDtypeStruct(shape, F32) for shape in outs],
        in_specs=[pl.BlockSpec(memory_space=space) for space in spaces],
        out_specs=[pl.BlockSpec(memory_space=pltpu.VMEM) for _ in outs],
        scratch_shapes=list(scratch),
        compiler_params=pltpu.CompilerParams(vmem_limit_bytes=VMEM_LIMIT),
    )(*args)


def in_hbm(*values):
    return [pltpu.with_memory_space_constraint(value, pltpu.HBM) for value in values]


def swap(value, axis, first, gap):
    pairs = []
    for i in range(16):
        partner = ((((i - first) % 16) ^ gap) + first) % 16
        pairs.append((i, partner))
    return lax.ppermute(value, axis, pairs)


def per_device(cell, frac, charge, count, fine, middle, coarse):
    packed = jnp.asarray(PACKED)
    ix, iy = lax.axis_index("gx"), lax.axis_index("gy")
    par = jnp.stack([ix & 1, (ix >> 1) & 1, iy & 1]).astype(jnp.int32)
    shat, mc, s1, s2, t1, t2, live = call(
        spread_kernel,
        [(17, 32, NZ), (9, 16, NZ), (5, 48, NZ), (5, 48, NZ), (16, NZ), (16, NZ), (1, 1, ATOMS)],
        (par, count, *in_hbm(cell, frac, charge)),
        [pltpu.SMEM] * 2 + [pltpu.HBM] * 3,
        [
            pltpu.VMEM((1, 1, ATOMS), jnp.int32),
            pltpu.VMEM((3, 1, 1, ATOMS), F32),
            pltpu.VMEM((1, 1, ATOMS), F32),
            pltpu.VMEM((288, (CX + 1) * 32), BF16),
            pltpu.VMEM((CX * CY, 4 * NZ), F32),
            pltpu.SemaphoreType.DMA((3,)),
        ],
    )
    r1 = swap(s1, "gx", 0, 1)
    r2 = swap(s2, "gx", 1, 1)
    rt1 = swap(t1, "gx", 0, 2)
    rt2 = swap(t2, "gx", 2, 2)
    (h,) = call(
        taps_kernel,
        [(KERNEL, 40, 256)],
        (*in_hbm(fine, middle, coarse, packed), live),
        [pltpu.HBM] * 4 + [pl.ANY],
        [
            pltpu.VMEM((KERNEL, KERNEL, KERNEL), F32),
            pltpu.VMEM((KERNEL, KERNEL, KERNEL), F32),
            pltpu.VMEM((KERNEL, KERNEL, KERNEL), F32),
            pltpu.VMEM((PACKED.shape[0] - PLACES["spread_high"][0], 256), BF16),
            pltpu.SemaphoreType.DMA((4,)),
        ],
    )
    e, g, y1, y2 = call(
        merge_kernel,
        [(25, 32, NZ), (17, 16, NZ), (42, 8, NZ), (42, 8, NZ)],
        (par, shat, mc, r1, r2, rt1, rt2, h),
        [pltpu.SMEM] + [pltpu.VMEM] * 6 + [pl.ANY],
    )
    q1 = swap(y1, "gy", 0, 1)
    q2 = swap(y2, "gy", 1, 1)
    pot, force = call(
        finish_kernel,
        [(CX, CY, NZ), (3, 1, 1, ATOMS)],
        (par, e, g, q1, q2, h, cell, frac, live, packed),
        [pltpu.SMEM] + [pltpu.VMEM] * 9,
        [
            pltpu.VMEM((25, 40, NZ), F32),
            pltpu.VMEM((17, 24, NZ), F32),
            pltpu.VMEM((25, 40, 256), F32),
            pltpu.VMEM((25, 40, 256), F32),
            pltpu.VMEM((18, 40, 256), F32),
            pltpu.VMEM((18, 32, 256), F32),
            pltpu.VMEM((CX + 1, 32, NZ), F32),
            pltpu.VMEM((4 * NZ, 2 * CX * CY), BF16),
        ],
    )
    return pot, force


def solution(mesh):
    return jax.shard_map(
        per_device,
        mesh=mesh,
        in_specs=(
            P("gx", "gy", None),
            P(None, "gx", "gy", None),
            P("gx", "gy", None),
            P("gx", "gy"),
            P(),
            P(),
            P(),
        ),
        out_specs=(P("gx", "gy", None), P(None, "gx", "gy", None)),
        check_vma=False,
    )
```

```python
import functools

import jax
import jax.numpy as jnp
import numpy as np
from jax import lax
from jax.experimental import pallas as pl
from jax.experimental.pallas import tpu as pltpu
from jax.sharding import PartitionSpec as P

CX = 16
CY = 24
NZ = 128
ATOMS = 4096
KERNEL = 9
TILE = 1024
HIGHEST = lax.Precision.HIGHEST
F32 = jnp.float32
BF16 = jnp.bfloat16
VMEM_LIMIT = 28 * 1024 * 1024


LINE = CY + KERNEL
FIRST = {128: 0, 64: 65, 32: 98}


def forward_table(n):
    z, k = np.arange(n)[:, None], np.arange(n // 2 + 1)[None, :]
    turn = np.exp(-2j * np.pi * k * z / n)
    return placed(turn, n)


def placed(turn, n):
    out = np.zeros((turn.shape[0], 256))
    first, count = FIRST[n], n // 2 + 1
    out[:, first : first + count] = turn.real
    out[:, 128 + first : 128 + first + count] = turn.imag
    return out


def inverse_table(n):
    z, k = np.arange(n)[:, None], np.arange(n // 2 + 1)[None, :]
    weight = np.where((k == 0) | (k == n // 2), 1.0, 2.0) / n
    return placed(weight * np.exp(-2j * np.pi * k * z / n), n).T


def tap_tables(n):
    c, k = np.arange(KERNEL)[:, None] - KERNEL // 2, np.arange(n // 2 + 1)[None, :]
    return placed(np.exp(2j * np.pi * k * c / n), n)


def line_tables():
    k = np.arange(LINE)
    forward = np.zeros((40, 40), complex)
    forward[:LINE, :LINE] = np.exp(-2j * np.pi * np.outer(k, k) / LINE)
    back = np.zeros((32, 40), complex)
    back[: CY + 1, :LINE] = np.exp(2j * np.pi * np.outer(np.arange(CY + 1), k) / LINE) / LINE
    spread = np.zeros((40, KERNEL), complex)
    spread[:LINE] = np.exp(2j * np.pi * np.outer(k, np.arange(KERNEL)) / LINE)

    def both(table, copies):
        return np.concatenate(
            [np.kron(np.eye(copies), table.real), np.kron(np.eye(copies), table.imag)], axis=0
        )

    return both(forward, 5), both(back, 6), both(spread, 1)


def restrict_z(n):
    out = np.zeros((n, n // 2))
    for i in range(n // 2):
        out[(2 * i - 1) % n, i] += 0.5
        out[2 * i, i] += 1.0
        out[(2 * i + 1) % n, i] += 0.5
    return out


def prolong_z(n):
    return restrict_z(2 * n).T


def tents(fine, step, coarse):
    far = np.abs(np.arange(fine)[None, :] - step * np.arange(coarse)[:, None])
    return np.maximum(0.0, 1.0 - far / step)


def plane_table(step):
    cx, cy = CX // step + 1, CY // step + 1
    along_x = tents(CX + 1, step, cx)
    along_y = tents(CY + 1, step, cy)
    out = np.zeros((9, 16, CX + 1, 32))
    out[:cx, :cy, :, : CY + 1] = along_x[:, None, :, None] * along_y[None, :, None, :]
    return out.reshape(144, (CX + 1) * 32)


def halves(table):
    table = np.asarray(table, np.float32)
    high = table.astype(BF16)
    return np.stack([high, (table - high.astype(np.float32)).astype(BF16)])


def tables():
    small = np.zeros((128, 256))
    small[:64] = forward_table(64)
    small[64:96] = forward_table(32)
    line, back, spread = line_tables()
    inverse = np.concatenate(
        [
            inverse_table(64) @ prolong_z(64),
            inverse_table(32) @ prolong_z(32) @ prolong_z(64),
        ],
        axis=1,
    )
    parts = {
        "plane2": np.asarray(plane_table(2).T, BF16),
        "plane4": np.asarray(plane_table(4).T, BF16),
    }
    for name, table in (
        ("forward", forward_table(128)),
        ("small", small),
        ("line", line),
        ("back", back),
        ("inverse", inverse_table(128)),
        ("levels", inverse),
        ("spread", spread),
        ("tap128", tap_tables(128)),
        ("tap64", tap_tables(64)),
        ("tap32", tap_tables(32)),
    ):
        parts[name + "_high"], parts[name + "_low"] = halves(table)
    places = {}
    blocks = []
    start = 0
    for name, part in parts.items():
        rows, cols = part.shape
        whole = -(-rows // 16) * 16
        places[name] = (start, whole, cols)
        blocks.append(np.pad(part, ((0, whole - rows), (0, 256 - cols))))
        start += whole
    return np.concatenate(blocks, axis=0), places


PACKED, PLACES = tables()


def table(ref, name, first=0):
    if name + "_high" in PLACES:
        return table(ref, name + "_high", first), table(ref, name + "_low", first)
    start, rows, cols = PLACES[name]
    return ref[start - first : start - first + rows, :cols]


def whole(ref, name, first):
    high, low = table(ref, name, first)
    return high.astype(F32) + low.astype(F32)


def dot(a, b):
    return jnp.dot(a, b, precision=HIGHEST, preferred_element_type=F32)


def dot_exact(table, value):
    high, low = split(value)
    return jnp.dot(table, high, preferred_element_type=F32) + jnp.dot(
        table, low, preferred_element_type=F32
    )


def split(value):
    high = value.astype(BF16)
    return high, (value - high.astype(F32)).astype(BF16)


def dot3(a, b):
    total = jnp.dot(a[0], b[0], preferred_element_type=F32)
    total += jnp.dot(a[0], b[1], preferred_element_type=F32)
    return total + jnp.dot(a[1], b[0], preferred_element_type=F32)


def tent(far, step):
    return jnp.maximum(step - jnp.abs(far), 0)


def plane_tents(step):
    row = lax.broadcasted_iota(jnp.int32, (144, (CX + 1) * 32), 0)
    col = lax.broadcasted_iota(jnp.int32, (144, (CX + 1) * 32), 1)
    along_x = tent((col >> 5) - step * (row >> 4), step)
    along_y = tent((col & 31) - step * (row & 15), step)
    return ((along_x * along_y).astype(F32) * (1.0 / step**2)).astype(BF16)


def depth_tents(step, first):
    row = lax.broadcasted_iota(jnp.int32, (NZ, NZ), 0)
    col = lax.broadcasted_iota(jnp.int32, (NZ, NZ), 1) - first
    far = (row - step * col) & (NZ - 1)
    weight = tent(far, step) + tent(NZ - far, step)
    weight = jnp.where((col >= 0) & (col < NZ // step), weight, 0)
    return (weight.astype(F32) * (1.0 / step)).astype(BF16)


def dot_right(value, table):
    high, low = split(value)
    return jnp.dot(high, table, preferred_element_type=F32) + jnp.dot(
        low, table, preferred_element_type=F32
    )


def coarse_lanes(shape):
    return lax.broadcasted_iota(jnp.int32, shape, len(shape) - 1) >= 64


def rows_of(cell_ref, frac_ref, charge_ref, t):
    span = pl.ds(t * TILE, TILE)
    cell = cell_ref[0, :, span]
    f = [frac_ref[k, 0, :, span] for k in range(3)]
    return cell, f, charge_ref[0, :, span], span


def one_hot(cell):
    row = lax.broadcasted_iota(jnp.int32, (CX * CY, TILE), 0)
    return jnp.where(row == (cell >> 7), 1.0, 0.0).astype(BF16)


def spread_kernel(
    par_ref, count_ref, cell_hbm, frac_hbm, charge_hbm,
    grid_ref, mc_ref, s1_ref, s2_ref, t1_ref, t2_ref, live_ref,
    cell_ref, frac_ref, charge_ref, planes_ref, acc_ref, sems,
):
    copies = [
        pltpu.make_async_copy(src, dst, sems.at[k])
        for k, (src, dst) in enumerate(
            (
                (cell_hbm, cell_ref),
                (frac_hbm, frac_ref),
                (charge_hbm, charge_ref),
            )
        )
    ]
    for copy in copies:
        copy.start()
    acc_ref[...] = jnp.zeros_like(acc_ref)
    grid_ref[...] = jnp.zeros_like(grid_ref)
    planes_ref[0:144] = plane_tents(2)
    planes_ref[144:288] = plane_tents(4)
    for copy in copies:
        copy.wait()
    slot = lax.broadcasted_iota(jnp.int32, (1, ATOMS), 1)
    live_ref[0] = jnp.where(slot < count_ref[0, 0], charge_ref[0], 0.0)

    def step(t, carry):
        cell, f, charge, _ = rows_of(cell_ref, frac_ref, live_ref, t)
        hot = one_hot(cell)
        z = cell & (NZ - 1)
        plane = lax.broadcasted_iota(jnp.int32, (NZ, TILE), 0)
        at_low = plane == z
        at_high = plane == ((z + 1) & (NZ - 1))
        wx = [1.0 - f[0], f[0]]
        wy = [1.0 - f[1], f[1]]
        wz = [1.0 - f[2], f[2]]
        low_hot = jnp.where(at_low, 1.0, 0.0).astype(BF16)
        high_hot = jnp.where(at_high, 1.0, 0.0).astype(BF16)
        highs = []
        lows = []
        for ab in range(4):
            flat = charge * wx[ab >> 1] * wy[ab & 1]
            weights = [flat * wz[e] for e in range(2)]
            tops = [w.astype(BF16).astype(F32) for w in weights]
            for group, (w0, w1) in (
                (highs, tops),
                (lows, [w - t for w, t in zip(weights, tops)]),
            ):
                group.append(low_hot * w0.astype(BF16) + high_hot * w1.astype(BF16))
        dims = (((1,), (1,)), ((), ()))
        acc_ref[...] += sum(
            lax.dot_general(
                hot, jnp.concatenate(group, axis=0), dims, preferred_element_type=F32
            )
            for group in (highs, lows)
        )
        return carry

    lax.fori_loop(0, ATOMS // TILE, step, 0, unroll=True)
    for ab in range(4):
        a, b = ab >> 1, ab & 1
        for x in range(CX):
            grid_ref[x + a, b : b + CY, :] += acc_ref[
                x * CY : (x + 1) * CY, ab * NZ : (ab + 1) * NZ
            ]
    grid = grid_ref[...].reshape((CX + 1) * 32, NZ)
    small = dot_exact(planes_ref[...], grid)
    mc = dot_right(small[:144], depth_tents(2, 0)) + dot_right(small[144:], depth_tents(4, 64))
    mc_ref[...] = mc.reshape(9, 16, NZ)

    even = par_ref[0] == 0
    even2 = par_ref[1] == 0
    is_coarse = coarse_lanes((5, 16, NZ))

    def put_low(ref):
        ref[:, :32, :] = grid_ref[0:5]
        ref[:, 32:, :] = mc_ref[0:5]

    def put_high(ref):
        ref[:, :32, :] = grid_ref[12:17]
        ref[:, 32:, :] = jnp.where(is_coarse, mc_ref[0:5], mc_ref[4:9])

    @pl.when(even)
    def _():
        put_high(s1_ref)
        put_low(s2_ref)

    @pl.when(jnp.logical_not(even))
    def _():
        put_low(s1_ref)
        put_high(s2_ref)

    @pl.when(even2)
    def _():
        t1_ref[...] = mc_ref[4]
        t2_ref[...] = mc_ref[0]

    @pl.when(jnp.logical_not(even2))
    def _():
        t1_ref[...] = mc_ref[0]
        t2_ref[...] = mc_ref[4]


def taps_kernel(
    fine_hbm, middle_hbm, coarse_hbm, packed_hbm, live_ref, h_ref,
    fine_ref, middle_ref, coarse_ref, packed_ref, sems,
):
    first = PLACES["spread_high"][0]
    pairs = (
        (fine_hbm, fine_ref),
        (middle_hbm, middle_ref),
        (coarse_hbm, coarse_ref),
        (packed_hbm.at[first : PACKED.shape[0]], packed_ref),
    )
    copies = [pltpu.make_async_copy(*pair, sems.at[k]) for k, pair in enumerate(pairs)]
    for copy in copies:
        copy.start()
    for copy in copies:
        copy.wait()
    levels = [
        (ref, whole(packed_ref, name, first)[:KERNEL])
        for ref, name in ((fine_ref, "tap128"), (middle_ref, "tap64"), (coarse_ref, "tap32"))
    ]
    spread = whole(packed_ref, "spread", first)
    for a in range(KERNEL):
        along_z = sum(dot(ref[a], tap) for ref, tap in levels)
        both = dot(spread, along_z)
        h_ref[a, :, :NZ] = both[:40, :NZ] - both[40:, NZ:]
        h_ref[a, :, NZ:] = both[:40, NZ:] + both[40:, :NZ]


def merge_kernel(
    par_ref, shat_ref, mc_ref, r1_ref, r2_ref, rt1_ref, rt2_ref, h_ref,
    e_ref, g_ref, s1_ref, s2_ref,
):
    e_ref[0:4] = jnp.zeros((4, 32, NZ), F32)
    e_ref[21:25] = jnp.zeros((4, 32, NZ), F32)
    e_ref[4:21] = shat_ref[...]
    g_ref[0:4] = jnp.zeros((4, 16, NZ), F32)
    g_ref[13:17] = jnp.zeros((4, 16, NZ), F32)
    g_ref[4:13] = mc_ref[...]
    is_coarse = coarse_lanes((5, 16, NZ))

    def merge(low_ref, high_ref):
        e_ref[0:5] += low_ref[:, :32, :]
        e_ref[20:25] += high_ref[:, :32, :]
        g_ref[0:5] += low_ref[:, 32:, :]
        high = high_ref[:, 32:, :]
        g_ref[12:17] += jnp.where(is_coarse, 0.0, high)
        g_ref[8:13] += jnp.where(is_coarse, high, 0.0)

    def merge2(low_ref, high_ref):
        g_ref[0] += jnp.where(is_coarse[0], low_ref[...], 0.0)
        g_ref[12] += jnp.where(is_coarse[0], high_ref[...], 0.0)

    even = par_ref[0] == 0
    even2 = par_ref[1] == 0

    @pl.when(even)
    def _():
        merge(r2_ref, r1_ref)

    @pl.when(jnp.logical_not(even))
    def _():
        merge(r1_ref, r2_ref)

    @pl.when(even2)
    def _():
        merge2(rt2_ref, rt1_ref)

    @pl.when(jnp.logical_not(even2))
    def _():
        merge2(rt1_ref, rt2_ref)

    def put_low(ref):
        ref[0:25] = e_ref[:, 0:8, :]
        ref[25:42] = g_ref[:, 0:8, :]

    def put_high(ref):
        ref[0:25, 0:5, :] = e_ref[:, 20:25, :]
        ref[0:25, 5:8, :] = jnp.zeros((25, 3, NZ), F32)
        ref[25:42] = jnp.where(
            coarse_lanes((17, 8, NZ)), g_ref[:, 2:10, :], g_ref[:, 8:16, :]
        )

    y_even = par_ref[2] == 0

    @pl.when(y_even)
    def _():
        put_high(s1_ref)
        put_low(s2_ref)

    @pl.when(jnp.logical_not(y_even))
    def _():
        put_low(s1_ref)
        put_high(s2_ref)


def hot_kernel(cell_ref, e_ref, hot_ref):
    def step(t, carry):
        span = pl.ds(pl.multiple_of(t * TILE, TILE), TILE)
        hot_ref[:, span] = one_hot(cell_ref[0, :, span])
        return carry

    lax.fori_loop(0, ATOMS // TILE, step, 0)


def finish_kernel(
    par_ref, e_ref, g_ref, r1_ref, r2_ref, h_ref, hot_ref, cell_ref, frac_ref, charge_ref, packed_ref,
    pot_ref, force_ref,
    ee_ref, gg_ref, z_ref, v_ref, o_ref, w_ref, full_ref, turned_ref,
):
    for ref, wide, src in ((ee_ref, 32, e_ref), (gg_ref, 16, g_ref)):
        ref[:, 0:4, :] = jnp.zeros((ref.shape[0], 4, NZ), F32)
        ref[:, 4 + wide :, :] = jnp.zeros((ref.shape[0], 4, NZ), F32)
        ref[:, 4 : 4 + wide, :] = src[...]
    is_coarse = coarse_lanes((17, 5, NZ))

    def merge(low_ref, high_ref):
        ee_ref[:, 0:5, :] += low_ref[0:25, 0:5, :]
        ee_ref[:, 28:33, :] += high_ref[0:25, 0:5, :]
        gg_ref[:, 0:5, :] += low_ref[25:42, 0:5, :]
        high = high_ref[25:42, 0:5, :]
        gg_ref[:, 16:21, :] += jnp.where(is_coarse, 0.0, high)
        gg_ref[:, 10:15, :] += jnp.where(is_coarse, high, 0.0)

    y_even = par_ref[2] == 0

    @pl.when(y_even)
    def _():
        merge(r2_ref, r1_ref)

    @pl.when(jnp.logical_not(y_even))
    def _():
        merge(r1_ref, r2_ref)

    z_ref[...] = dot3(split(ee_ref[...].reshape(1000, NZ)), table(packed_ref, "forward")).reshape(25, 40, 256)
    z_ref[0:17, 0:24, :] += dot3(split(gg_ref[...].reshape(408, NZ)), table(packed_ref, "small")).reshape(
        17, 24, 256
    )
    for group in range(5):
        rows = slice(5 * group, 5 * group + 5)
        both = dot3(table(packed_ref, "line"), split(z_ref[rows].reshape(200, 256)))
        v_ref[rows, :, :NZ] = (both[:200, :NZ] - both[200:, NZ:]).reshape(5, 40, NZ)
        v_ref[rows, :, NZ:] = (both[:200, NZ:] + both[200:, :NZ]).reshape(5, 40, NZ)

    o_ref[CX + 1] = jnp.zeros((40, 256), F32)

    def across(t, carry):
        rows = pl.ds(pl.multiple_of(t * 8, 8), 8)
        for part in range(2):
            acc = [jnp.zeros((8, NZ), F32) for _ in range(CX + 1)]
            for xin in range(CX + KERNEL):
                real = v_ref[xin, rows, :NZ]
                imag = v_ref[xin, rows, NZ:]
                for a in range(KERNEL):
                    x = xin - a
                    if 0 <= x <= CX:
                        h_real = h_ref[a, rows, :NZ]
                        h_imag = h_ref[a, rows, NZ:]
                        if part == 0:
                            acc[x] = acc[x] + real * h_real - imag * h_imag
                        else:
                            acc[x] = acc[x] + real * h_imag + imag * h_real
            for x in range(CX + 1):
                o_ref[x, rows, part * NZ : (part + 1) * NZ] = acc[x]
        return carry

    lax.fori_loop(0, 5, across, 0)
    for group in range(3):
        rows = slice(6 * group, 6 * group + 6)
        both = dot3(table(packed_ref, "back"), split(o_ref[rows].reshape(240, 256)))
        w_ref[rows, :, :NZ] = (both[:192, :NZ] - both[192:, NZ:]).reshape(6, 32, NZ)
        w_ref[rows, :, NZ:] = (both[:192, NZ:] + both[192:, :NZ]).reshape(6, 32, NZ)
    both = dot3(split(w_ref[0:9, 0:16, :].reshape(144, 256)), table(packed_ref, "levels"))
    full = dot3(split(w_ref[0 : CX + 1].reshape((CX + 1) * 32, 256)), table(packed_ref, "inverse"))
    for k, name in enumerate(("plane2", "plane4")):
        full += dot_exact(table(packed_ref, name), both[:, k * NZ : (k + 1) * NZ])
    full_ref[...] = full.reshape(CX + 1, 32, NZ)
    pot_ref[...] = full_ref[0:CX, 0:CY, :]
    for ab in range(4):
        a, b = ab >> 1, ab & 1
        part = full_ref[a : a + CX, b : b + CY, :].reshape(CX * CY, NZ).T
        high, low = split(part)
        turned_ref[ab * NZ : (ab + 1) * NZ, : CX * CY] = high
        turned_ref[ab * NZ : (ab + 1) * NZ, CX * CY :] = low

    def step(t, carry):
        cell, f, charge, span = rows_of(cell_ref, frac_ref, charge_ref, t)
        hot = hot_ref[:, span]
        hot = jnp.concatenate([hot, hot], axis=0)
        z = cell & (NZ - 1)
        plane = lax.broadcasted_iota(jnp.int32, (NZ, TILE), 0)
        at_low = plane == z
        at_high = plane == ((z + 1) & (NZ - 1))
        corner = []
        for ab in range(4):
            rows = slice(ab * NZ, (ab + 1) * NZ)
            found = jnp.dot(turned_ref[rows, :], hot, preferred_element_type=F32)
            corner.append(
                [
                    jnp.sum(jnp.where(mask, found, 0.0), axis=0, keepdims=True)
                    for mask in (at_low, at_high)
                ]
            )
        wx = [1.0 - f[0], f[0]]
        wy = [1.0 - f[1], f[1]]
        wz = [1.0 - f[2], f[2]]
        sign = [-1.0, 1.0]
        sums = [0.0, 0.0, 0.0]
        for a in range(2):
            for b in range(2):
                for e in range(2):
                    v = corner[2 * a + b][e]
                    sums[0] = sums[0] + sign[a] * wy[b] * wz[e] * v
                    sums[1] = sums[1] + wx[a] * sign[b] * wz[e] * v
                    sums[2] = sums[2] + wx[a] * wy[b] * sign[e] * v
        for k in range(3):
            force_ref[k, 0, :, span] = -charge * sums[k]
        return carry

    lax.fori_loop(0, ATOMS // TILE, step, 0)


def call(kernel, outs, args, spaces, scratch=(), dtype=F32):
    return pl.pallas_call(
        kernel,
        out_shape=[jax.ShapeDtypeStruct(shape, dtype) for shape in outs],
        in_specs=[pl.BlockSpec(memory_space=space) for space in spaces],
        out_specs=[pl.BlockSpec(memory_space=pltpu.VMEM) for _ in outs],
        scratch_shapes=list(scratch),
        compiler_params=pltpu.CompilerParams(vmem_limit_bytes=VMEM_LIMIT),
    )(*args)


def in_hbm(*values):
    return [pltpu.with_memory_space_constraint(value, pltpu.HBM) for value in values]


def swap(value, axis, first, gap):
    pairs = []
    for i in range(16):
        partner = ((((i - first) % 16) ^ gap) + first) % 16
        pairs.append((i, partner))
    return lax.ppermute(value, axis, pairs)


def per_device(cell, frac, charge, count, fine, middle, coarse):
    packed = jnp.asarray(PACKED)
    ix, iy = lax.axis_index("gx"), lax.axis_index("gy")
    par = jnp.stack([ix & 1, (ix >> 1) & 1, iy & 1]).astype(jnp.int32)
    shat, mc, s1, s2, t1, t2, live = call(
        spread_kernel,
        [(17, 32, NZ), (9, 16, NZ), (5, 48, NZ), (5, 48, NZ), (16, NZ), (16, NZ), (1, 1, ATOMS)],
        (par, count, *in_hbm(cell, frac, charge)),
        [pltpu.SMEM] * 2 + [pltpu.HBM] * 3,
        [
            pltpu.VMEM((1, 1, ATOMS), jnp.int32),
            pltpu.VMEM((3, 1, 1, ATOMS), F32),
            pltpu.VMEM((1, 1, ATOMS), F32),
            pltpu.VMEM((288, (CX + 1) * 32), BF16),
            pltpu.VMEM((CX * CY, 4 * NZ), F32),
            pltpu.SemaphoreType.DMA((3,)),
        ],
    )
    r1 = swap(s1, "gx", 0, 1)
    r2 = swap(s2, "gx", 1, 1)
    rt1 = swap(t1, "gx", 0, 2)
    rt2 = swap(t2, "gx", 2, 2)
    (h,) = call(
        taps_kernel,
        [(KERNEL, 40, 256)],
        (*in_hbm(fine, middle, coarse, packed), live),
        [pltpu.HBM] * 4 + [pl.ANY],
        [
            pltpu.VMEM((KERNEL, KERNEL, KERNEL), F32),
            pltpu.VMEM((KERNEL, KERNEL, KERNEL), F32),
            pltpu.VMEM((KERNEL, KERNEL, KERNEL), F32),
            pltpu.VMEM((PACKED.shape[0] - PLACES["spread_high"][0], 256), BF16),
            pltpu.SemaphoreType.DMA((4,)),
        ],
    )
    e, g, y1, y2 = call(
        merge_kernel,
        [(25, 32, NZ), (17, 16, NZ), (42, 8, NZ), (42, 8, NZ)],
        (par, shat, mc, r1, r2, rt1, rt2, h),
        [pltpu.SMEM] + [pltpu.VMEM] * 6 + [pl.ANY],
    )
    q1 = swap(y1, "gy", 0, 1)
    q2 = swap(y2, "gy", 1, 1)
    (hot,) = call(
        hot_kernel, [(CX * CY, ATOMS)], (cell, e), [pltpu.VMEM, pl.ANY], dtype=BF16
    )
    pot, force = call(
        finish_kernel,
        [(CX, CY, NZ), (3, 1, 1, ATOMS)],
        (par, e, g, q1, q2, h, hot, cell, frac, live, packed),
        [pltpu.SMEM] + [pltpu.VMEM] * 10,
        [
            pltpu.VMEM((25, 40, NZ), F32),
            pltpu.VMEM((17, 24, NZ), F32),
            pltpu.VMEM((25, 40, 256), F32),
            pltpu.VMEM((25, 40, 256), F32),
            pltpu.VMEM((18, 40, 256), F32),
            pltpu.VMEM((18, 32, 256), F32),
            pltpu.VMEM((CX + 1, 32, NZ), F32),
            pltpu.VMEM((4 * NZ, 2 * CX * CY), BF16),
        ],
    )
    return pot, force


def solution(mesh):
    return jax.shard_map(
        per_device,
        mesh=mesh,
        in_specs=(
            P("gx", "gy", None),
            P(None, "gx", "gy", None),
            P("gx", "gy", None),
            P("gx", "gy"),
            P(),
            P(),
            P(),
        ),
        out_specs=(P("gx", "gy", None), P(None, "gx", "gy", None)),
        check_vma=False,
    )
```

```python
import functools

import jax
import jax.numpy as jnp
import numpy as np
from jax import lax
from jax.experimental import pallas as pl
from jax.experimental.pallas import tpu as pltpu
from jax.sharding import PartitionSpec as P

CX = 16
CY = 24
NZ = 128
ATOMS = 4096
KERNEL = 9
TILE = 1024
HIGHEST = lax.Precision.HIGHEST
F32 = jnp.float32
BF16 = jnp.bfloat16
VMEM_LIMIT = 28 * 1024 * 1024


LINE = CY + KERNEL
FIRST = {128: 0, 64: 65, 32: 98}


def forward_table(n):
    z, k = np.arange(n)[:, None], np.arange(n // 2 + 1)[None, :]
    turn = np.exp(-2j * np.pi * k * z / n)
    return placed(turn, n)


def placed(turn, n):
    out = np.zeros((turn.shape[0], 256))
    first, count = FIRST[n], n // 2 + 1
    out[:, first : first + count] = turn.real
    out[:, 128 + first : 128 + first + count] = turn.imag
    return out


def inverse_table(n):
    z, k = np.arange(n)[:, None], np.arange(n // 2 + 1)[None, :]
    weight = np.where((k == 0) | (k == n // 2), 1.0, 2.0) / n
    return placed(weight * np.exp(-2j * np.pi * k * z / n), n).T


def tap_tables(n):
    c, k = np.arange(KERNEL)[:, None] - KERNEL // 2, np.arange(n // 2 + 1)[None, :]
    return placed(np.exp(2j * np.pi * k * c / n), n)


def line_tables():
    k = np.arange(LINE)
    forward = np.zeros((40, 40), complex)
    forward[:LINE, :LINE] = np.exp(-2j * np.pi * np.outer(k, k) / LINE)
    back = np.zeros((32, 40), complex)
    back[: CY + 1, :LINE] = np.exp(2j * np.pi * np.outer(np.arange(CY + 1), k) / LINE) / LINE
    spread = np.zeros((40, KERNEL), complex)
    spread[:LINE] = np.exp(2j * np.pi * np.outer(k, np.arange(KERNEL)) / LINE)

    def both(table, copies):
        return np.concatenate(
            [np.kron(np.eye(copies), table.real), np.kron(np.eye(copies), table.imag)], axis=0
        )

    return both(forward, 5), both(back, 6), both(spread, 1)


def restrict_z(n):
    out = np.zeros((n, n // 2))
    for i in range(n // 2):
        out[(2 * i - 1) % n, i] += 0.5
        out[2 * i, i] += 1.0
        out[(2 * i + 1) % n, i] += 0.5
    return out


def prolong_z(n):
    return restrict_z(2 * n).T


def tents(fine, step, coarse):
    far = np.abs(np.arange(fine)[None, :] - step * np.arange(coarse)[:, None])
    return np.maximum(0.0, 1.0 - far / step)


def plane_table(step):
    cx, cy = CX // step + 1, CY // step + 1
    along_x = tents(CX + 1, step, cx)
    along_y = tents(CY + 1, step, cy)
    out = np.zeros((9, 16, CX + 1, 32))
    out[:cx, :cy, :, : CY + 1] = along_x[:, None, :, None] * along_y[None, :, None, :]
    return out.reshape(144, (CX + 1) * 32)


def halves(table):
    table = np.asarray(table, np.float32)
    high = table.astype(BF16)
    return np.stack([high, (table - high.astype(np.float32)).astype(BF16)])


def tables():
    small = np.zeros((128, 256))
    small[:64] = forward_table(64)
    small[64:96] = forward_table(32)
    line, back, spread = line_tables()
    inverse = np.concatenate(
        [
            inverse_table(64) @ prolong_z(64),
            inverse_table(32) @ prolong_z(32) @ prolong_z(64),
        ],
        axis=1,
    )
    parts = {
        "plane2": np.asarray(plane_table(2).T, BF16),
        "plane4": np.asarray(plane_table(4).T, BF16),
    }
    for name, table in (
        ("forward", forward_table(128)),
        ("small", small),
        ("line", line),
        ("back", back),
        ("inverse", inverse_table(128)),
        ("levels", inverse),
        ("spread", spread),
        ("tap128", tap_tables(128)),
        ("tap64", tap_tables(64)),
        ("tap32", tap_tables(32)),
    ):
        parts[name + "_high"], parts[name + "_low"] = halves(table)
    places = {}
    blocks = []
    start = 0
    for name, part in parts.items():
        rows, cols = part.shape
        whole = -(-rows // 16) * 16
        places[name] = (start, whole, cols)
        blocks.append(np.pad(part, ((0, whole - rows), (0, 256 - cols))))
        start += whole
    return np.concatenate(blocks, axis=0), places


PACKED, PLACES = tables()


def table(ref, name, first=0):
    if name + "_high" in PLACES:
        return table(ref, name + "_high", first), table(ref, name + "_low", first)
    start, rows, cols = PLACES[name]
    return ref[start - first : start - first + rows, :cols]


def whole(ref, name, first):
    high, low = table(ref, name, first)
    return high.astype(F32) + low.astype(F32)


def dot(a, b):
    return jnp.dot(a, b, precision=HIGHEST, preferred_element_type=F32)


def dot_exact(table, value):
    high, low = split(value)
    return jnp.dot(table, high, preferred_element_type=F32) + jnp.dot(
        table, low, preferred_element_type=F32
    )


def split(value):
    high = value.astype(BF16)
    return high, (value - high.astype(F32)).astype(BF16)


def dot3(a, b):
    total = jnp.dot(a[0], b[0], preferred_element_type=F32)
    total += jnp.dot(a[0], b[1], preferred_element_type=F32)
    return total + jnp.dot(a[1], b[0], preferred_element_type=F32)


def tent(far, step):
    return jnp.maximum(step - jnp.abs(far), 0)


def plane_tents(step):
    row = lax.broadcasted_iota(jnp.int32, (144, (CX + 1) * 32), 0)
    col = lax.broadcasted_iota(jnp.int32, (144, (CX + 1) * 32), 1)
    along_x = tent((col >> 5) - step * (row >> 4), step)
    along_y = tent((col & 31) - step * (row & 15), step)
    return ((along_x * along_y).astype(F32) * (1.0 / step**2)).astype(BF16)


def depth_tents(step, first):
    row = lax.broadcasted_iota(jnp.int32, (NZ, NZ), 0)
    col = lax.broadcasted_iota(jnp.int32, (NZ, NZ), 1) - first
    far = (row - step * col) & (NZ - 1)
    weight = tent(far, step) + tent(NZ - far, step)
    weight = jnp.where((col >= 0) & (col < NZ // step), weight, 0)
    return (weight.astype(F32) * (1.0 / step)).astype(BF16)


def dot_right(value, table):
    high, low = split(value)
    return jnp.dot(high, table, preferred_element_type=F32) + jnp.dot(
        low, table, preferred_element_type=F32
    )


def coarse_lanes(shape):
    return lax.broadcasted_iota(jnp.int32, shape, len(shape) - 1) >= 64


def rows_of(cell_ref, frac_ref, charge_ref, t):
    span = pl.ds(t * TILE, TILE)
    cell = cell_ref[0, :, span]
    f = [frac_ref[k, 0, :, span] for k in range(3)]
    return cell, f, charge_ref[0, :, span], span


def one_hot(cell):
    row = lax.broadcasted_iota(jnp.int32, (CX * CY, TILE), 0)
    return jnp.where(row == (cell >> 7), 1.0, 0.0).astype(BF16)


def spread_kernel(
    par_ref, count_ref, cell_hbm, frac_hbm, charge_hbm,
    grid_ref, mc_ref, s1_ref, s2_ref, t1_ref, t2_ref, live_ref,
    cell_ref, frac_ref, charge_ref, planes_ref, acc_ref, sems,
):
    copies = [
        pltpu.make_async_copy(src, dst, sems.at[k])
        for k, (src, dst) in enumerate(
            (
                (cell_hbm, cell_ref),
                (frac_hbm, frac_ref),
                (charge_hbm, charge_ref),
            )
        )
    ]
    for copy in copies:
        copy.start()
    acc_ref[...] = jnp.zeros_like(acc_ref)
    grid_ref[...] = jnp.zeros_like(grid_ref)
    planes_ref[0:144] = plane_tents(2)
    planes_ref[144:288] = plane_tents(4)
    for copy in copies:
        copy.wait()
    slot = lax.broadcasted_iota(jnp.int32, (1, ATOMS), 1)
    live_ref[0] = jnp.where(slot < count_ref[0, 0], charge_ref[0], 0.0)

    def step(t, carry):
        cell, f, charge, _ = rows_of(cell_ref, frac_ref, live_ref, t)
        hot = one_hot(cell)
        z = cell & (NZ - 1)
        plane = lax.broadcasted_iota(jnp.int32, (NZ, TILE), 0)
        at_low = plane == z
        at_high = plane == ((z + 1) & (NZ - 1))
        wx = [1.0 - f[0], f[0]]
        wy = [1.0 - f[1], f[1]]
        wz = [1.0 - f[2], f[2]]
        low_hot = jnp.where(at_low, 1.0, 0.0).astype(BF16)
        high_hot = jnp.where(at_high, 1.0, 0.0).astype(BF16)
        highs = []
        lows = []
        for ab in range(4):
            flat = charge * wx[ab >> 1] * wy[ab & 1]
            weights = [flat * wz[e] for e in range(2)]
            tops = [w.astype(BF16).astype(F32) for w in weights]
            for group, (w0, w1) in (
                (highs, tops),
                (lows, [w - t for w, t in zip(weights, tops)]),
            ):
                group.append(low_hot * w0.astype(BF16) + high_hot * w1.astype(BF16))
        dims = (((1,), (1,)), ((), ()))
        acc_ref[...] += sum(
            lax.dot_general(
                hot, jnp.concatenate(group, axis=0), dims, preferred_element_type=F32
            )
            for group in (highs, lows)
        )
        return carry

    lax.fori_loop(0, ATOMS // TILE, step, 0, unroll=True)
    for ab in range(4):
        a, b = ab >> 1, ab & 1
        for x in range(CX):
            grid_ref[x + a, b : b + CY, :] += acc_ref[
                x * CY : (x + 1) * CY, ab * NZ : (ab + 1) * NZ
            ]
    grid = grid_ref[...].reshape((CX + 1) * 32, NZ)
    small = dot_exact(planes_ref[...], grid)
    mc = dot_right(small[:144], depth_tents(2, 0)) + dot_right(small[144:], depth_tents(4, 64))
    mc_ref[...] = mc.reshape(9, 16, NZ)

    even = par_ref[0] == 0
    even2 = par_ref[1] == 0
    is_coarse = coarse_lanes((5, 16, NZ))

    def put_low(ref):
        ref[:, :32, :] = grid_ref[0:5]
        ref[:, 32:, :] = mc_ref[0:5]

    def put_high(ref):
        ref[:, :32, :] = grid_ref[12:17]
        ref[:, 32:, :] = jnp.where(is_coarse, mc_ref[0:5], mc_ref[4:9])

    @pl.when(even)
    def _():
        put_high(s1_ref)
        put_low(s2_ref)

    @pl.when(jnp.logical_not(even))
    def _():
        put_low(s1_ref)
        put_high(s2_ref)

    @pl.when(even2)
    def _():
        t1_ref[...] = mc_ref[4]
        t2_ref[...] = mc_ref[0]

    @pl.when(jnp.logical_not(even2))
    def _():
        t1_ref[...] = mc_ref[0]
        t2_ref[...] = mc_ref[4]


def taps_kernel(
    fine_hbm, middle_hbm, coarse_hbm, packed_hbm, live_ref, h_ref,
    fine_ref, middle_ref, coarse_ref, packed_ref, sems,
):
    first = PLACES["spread_high"][0]
    pairs = (
        (fine_hbm, fine_ref),
        (middle_hbm, middle_ref),
        (coarse_hbm, coarse_ref),
        (packed_hbm.at[first : PACKED.shape[0]], packed_ref),
    )
    copies = [pltpu.make_async_copy(*pair, sems.at[k]) for k, pair in enumerate(pairs)]
    for copy in copies:
        copy.start()
    for copy in copies:
        copy.wait()
    levels = [
        (ref, whole(packed_ref, name, first)[:KERNEL])
        for ref, name in ((fine_ref, "tap128"), (middle_ref, "tap64"), (coarse_ref, "tap32"))
    ]
    spread = whole(packed_ref, "spread", first)
    for a in range(KERNEL):
        along_z = sum(dot(ref[a], tap) for ref, tap in levels)
        both = dot(spread, along_z)
        h_ref[a, :, :NZ] = both[:40, :NZ] - both[40:, NZ:]
        h_ref[a, :, NZ:] = both[:40, NZ:] + both[40:, :NZ]


def merge_kernel(
    par_ref, shat_ref, mc_ref, r1_ref, r2_ref, rt1_ref, rt2_ref, h_ref,
    e_ref, g_ref, s1_ref, s2_ref,
):
    e_ref[0:4] = jnp.zeros((4, 32, NZ), F32)
    e_ref[21:25] = jnp.zeros((4, 32, NZ), F32)
    e_ref[4:21] = shat_ref[...]
    g_ref[0:4] = jnp.zeros((4, 16, NZ), F32)
    g_ref[13:17] = jnp.zeros((4, 16, NZ), F32)
    g_ref[4:13] = mc_ref[...]
    is_coarse = coarse_lanes((5, 16, NZ))

    def merge(low_ref, high_ref):
        e_ref[0:5] += low_ref[:, :32, :]
        e_ref[20:25] += high_ref[:, :32, :]
        g_ref[0:5] += low_ref[:, 32:, :]
        high = high_ref[:, 32:, :]
        g_ref[12:17] += jnp.where(is_coarse, 0.0, high)
        g_ref[8:13] += jnp.where(is_coarse, high, 0.0)

    def merge2(low_ref, high_ref):
        g_ref[0] += jnp.where(is_coarse[0], low_ref[...], 0.0)
        g_ref[12] += jnp.where(is_coarse[0], high_ref[...], 0.0)

    even = par_ref[0] == 0
    even2 = par_ref[1] == 0

    @pl.when(even)
    def _():
        merge(r2_ref, r1_ref)

    @pl.when(jnp.logical_not(even))
    def _():
        merge(r1_ref, r2_ref)

    @pl.when(even2)
    def _():
        merge2(rt2_ref, rt1_ref)

    @pl.when(jnp.logical_not(even2))
    def _():
        merge2(rt1_ref, rt2_ref)

    def put_low(ref):
        ref[0:25] = e_ref[:, 0:8, :]
        ref[25:42] = g_ref[:, 0:8, :]

    def put_high(ref):
        ref[0:25, 0:5, :] = e_ref[:, 20:25, :]
        ref[0:25, 5:8, :] = jnp.zeros((25, 3, NZ), F32)
        ref[25:42] = jnp.where(
            coarse_lanes((17, 8, NZ)), g_ref[:, 2:10, :], g_ref[:, 8:16, :]
        )

    y_even = par_ref[2] == 0

    @pl.when(y_even)
    def _():
        put_high(s1_ref)
        put_low(s2_ref)

    @pl.when(jnp.logical_not(y_even))
    def _():
        put_low(s1_ref)
        put_high(s2_ref)


def hot_kernel(cell_ref, e_ref, hot_ref):
    def step(t, carry):
        span = pl.ds(pl.multiple_of(t * TILE, TILE), TILE)
        hot_ref[:, span] = one_hot(cell_ref[0, :, span])
        return carry

    lax.fori_loop(0, ATOMS // TILE, step, 0)


def finish_kernel(
    par_ref, e_ref, g_ref, r1_ref, r2_ref, h_ref, hot_ref, cell_ref, frac_ref, charge_ref, packed_ref,
    pot_ref, force_ref,
    ee_ref, gg_ref, z_ref, v_ref, o_ref, w_ref, full_ref, turned_ref,
):
    for ref, wide, src in ((ee_ref, 32, e_ref), (gg_ref, 16, g_ref)):
        ref[:, 0:4, :] = jnp.zeros((ref.shape[0], 4, NZ), F32)
        ref[:, 4 + wide :, :] = jnp.zeros((ref.shape[0], 4, NZ), F32)
        ref[:, 4 : 4 + wide, :] = src[...]
    is_coarse = coarse_lanes((17, 5, NZ))

    def merge(low_ref, high_ref):
        ee_ref[:, 0:5, :] += low_ref[0:25, 0:5, :]
        ee_ref[:, 28:33, :] += high_ref[0:25, 0:5, :]
        gg_ref[:, 0:5, :] += low_ref[25:42, 0:5, :]
        high = high_ref[25:42, 0:5, :]
        gg_ref[:, 16:21, :] += jnp.where(is_coarse, 0.0, high)
        gg_ref[:, 10:15, :] += jnp.where(is_coarse, high, 0.0)

    y_even = par_ref[2] == 0

    @pl.when(y_even)
    def _():
        merge(r2_ref, r1_ref)

    @pl.when(jnp.logical_not(y_even))
    def _():
        merge(r1_ref, r2_ref)

    z_ref[...] = dot3(split(ee_ref[...].reshape(1000, NZ)), table(packed_ref, "forward")).reshape(25, 40, 256)
    z_ref[0:17, 0:24, :] += dot3(split(gg_ref[...].reshape(408, NZ)), table(packed_ref, "small")).reshape(
        17, 24, 256
    )
    for group in range(5):
        rows = slice(5 * group, 5 * group + 5)
        both = dot3(table(packed_ref, "line"), split(z_ref[rows].reshape(200, 256)))
        v_ref[rows, :, :NZ] = (both[:200, :NZ] - both[200:, NZ:]).reshape(5, 40, NZ)
        v_ref[rows, :, NZ:] = (both[:200, NZ:] + both[200:, :NZ]).reshape(5, 40, NZ)

    o_ref[CX + 1] = jnp.zeros((40, 256), F32)

    def across(t, carry):
        rows = pl.ds(pl.multiple_of(t * 8, 8), 8)
        for part in range(2):
            acc = [jnp.zeros((8, NZ), F32) for _ in range(CX + 1)]
            for xin in range(CX + KERNEL):
                real = v_ref[xin, rows, :NZ]
                imag = v_ref[xin, rows, NZ:]
                for a in range(KERNEL):
                    x = xin - a
                    if 0 <= x <= CX:
                        h_real = h_ref[a, rows, :NZ]
                        h_imag = h_ref[a, rows, NZ:]
                        if part == 0:
                            acc[x] = acc[x] + real * h_real - imag * h_imag
                        else:
                            acc[x] = acc[x] + real * h_imag + imag * h_real
            for x in range(CX + 1):
                o_ref[x, rows, part * NZ : (part + 1) * NZ] = acc[x]
        return carry

    lax.fori_loop(0, 5, across, 0)
    for group in range(3):
        rows = slice(6 * group, 6 * group + 6)
        both = dot3(table(packed_ref, "back"), split(o_ref[rows].reshape(240, 256)))
        w_ref[rows, :, :NZ] = (both[:192, :NZ] - both[192:, NZ:]).reshape(6, 32, NZ)
        w_ref[rows, :, NZ:] = (both[:192, NZ:] + both[192:, :NZ]).reshape(6, 32, NZ)
    both = dot3(split(w_ref[0:9, 0:16, :].reshape(144, 256)), table(packed_ref, "levels"))
    full = dot3(split(w_ref[0 : CX + 1].reshape((CX + 1) * 32, 256)), table(packed_ref, "inverse"))
    for k, name in enumerate(("plane2", "plane4")):
        full += dot_exact(table(packed_ref, name), both[:, k * NZ : (k + 1) * NZ])
    full_ref[...] = full.reshape(CX + 1, 32, NZ)
    pot_ref[...] = full_ref[0:CX, 0:CY, :]
    for ab in range(4):
        a, b = ab >> 1, ab & 1
        part = full_ref[a : a + CX, b : b + CY, :].reshape(CX * CY, NZ).T
        high, low = split(part)
        turned_ref[ab * NZ : (ab + 1) * NZ, : CX * CY] = high
        turned_ref[ab * NZ : (ab + 1) * NZ, CX * CY :] = low

    def step(t, carry):
        cell, f, charge, span = rows_of(cell_ref, frac_ref, charge_ref, t)
        hot = hot_ref[:, span]
        hot = jnp.concatenate([hot, hot], axis=0)
        z = cell & (NZ - 1)
        plane = lax.broadcasted_iota(jnp.int32, (NZ, TILE), 0)
        at_low = plane == z
        at_high = plane == ((z + 1) & (NZ - 1))
        corner = []
        for ab in range(4):
            rows = slice(ab * NZ, (ab + 1) * NZ)
            found = jnp.dot(turned_ref[rows, :], hot, preferred_element_type=F32)
            corner.append(
                [
                    jnp.sum(jnp.where(mask, found, 0.0), axis=0, keepdims=True)
                    for mask in (at_low, at_high)
                ]
            )
        wx = [1.0 - f[0], f[0]]
        wy = [1.0 - f[1], f[1]]
        wz = [1.0 - f[2], f[2]]
        sign = [-1.0, 1.0]
        sums = [0.0, 0.0, 0.0]
        for a in range(2):
            for b in range(2):
                for e in range(2):
                    v = corner[2 * a + b][e]
                    sums[0] = sums[0] + sign[a] * wy[b] * wz[e] * v
                    sums[1] = sums[1] + wx[a] * sign[b] * wz[e] * v
                    sums[2] = sums[2] + wx[a] * wy[b] * sign[e] * v
        for k in range(3):
            force_ref[k, 0, :, span] = -charge * sums[k]
        return carry

    lax.fori_loop(0, ATOMS // TILE, step, 0, unroll=True)


def call(kernel, outs, args, spaces, scratch=(), dtype=F32):
    return pl.pallas_call(
        kernel,
        out_shape=[jax.ShapeDtypeStruct(shape, dtype) for shape in outs],
        in_specs=[pl.BlockSpec(memory_space=space) for space in spaces],
        out_specs=[pl.BlockSpec(memory_space=pltpu.VMEM) for _ in outs],
        scratch_shapes=list(scratch),
        compiler_params=pltpu.CompilerParams(vmem_limit_bytes=VMEM_LIMIT),
    )(*args)


def in_hbm(*values):
    return [pltpu.with_memory_space_constraint(value, pltpu.HBM) for value in values]


def swap(value, axis, first, gap):
    pairs = []
    for i in range(16):
        partner = ((((i - first) % 16) ^ gap) + first) % 16
        pairs.append((i, partner))
    return lax.ppermute(value, axis, pairs)


def per_device(cell, frac, charge, count, fine, middle, coarse):
    packed = jnp.asarray(PACKED)
    ix, iy = lax.axis_index("gx"), lax.axis_index("gy")
    par = jnp.stack([ix & 1, (ix >> 1) & 1, iy & 1]).astype(jnp.int32)
    shat, mc, s1, s2, t1, t2, live = call(
        spread_kernel,
        [(17, 32, NZ), (9, 16, NZ), (5, 48, NZ), (5, 48, NZ), (16, NZ), (16, NZ), (1, 1, ATOMS)],
        (par, count, *in_hbm(cell, frac, charge)),
        [pltpu.SMEM] * 2 + [pltpu.HBM] * 3,
        [
            pltpu.VMEM((1, 1, ATOMS), jnp.int32),
            pltpu.VMEM((3, 1, 1, ATOMS), F32),
            pltpu.VMEM((1, 1, ATOMS), F32),
            pltpu.VMEM((288, (CX + 1) * 32), BF16),
            pltpu.VMEM((CX * CY, 4 * NZ), F32),
            pltpu.SemaphoreType.DMA((3,)),
        ],
    )
    r1 = swap(s1, "gx", 0, 1)
    r2 = swap(s2, "gx", 1, 1)
    rt1 = swap(t1, "gx", 0, 2)
    rt2 = swap(t2, "gx", 2, 2)
    (h,) = call(
        taps_kernel,
        [(KERNEL, 40, 256)],
        (*in_hbm(fine, middle, coarse, packed), live),
        [pltpu.HBM] * 4 + [pl.ANY],
        [
            pltpu.VMEM((KERNEL, KERNEL, KERNEL), F32),
            pltpu.VMEM((KERNEL, KERNEL, KERNEL), F32),
            pltpu.VMEM((KERNEL, KERNEL, KERNEL), F32),
            pltpu.VMEM((PACKED.shape[0] - PLACES["spread_high"][0], 256), BF16),
            pltpu.SemaphoreType.DMA((4,)),
        ],
    )
    e, g, y1, y2 = call(
        merge_kernel,
        [(25, 32, NZ), (17, 16, NZ), (42, 8, NZ), (42, 8, NZ)],
        (par, shat, mc, r1, r2, rt1, rt2, h),
        [pltpu.SMEM] + [pltpu.VMEM] * 6 + [pl.ANY],
    )
    q1 = swap(y1, "gy", 0, 1)
    q2 = swap(y2, "gy", 1, 1)
    (hot,) = call(
        hot_kernel, [(CX * CY, ATOMS)], (cell, e), [pltpu.VMEM, pl.ANY], dtype=BF16
    )
    pot, force = call(
        finish_kernel,
        [(CX, CY, NZ), (3, 1, 1, ATOMS)],
        (par, e, g, q1, q2, h, hot, cell, frac, live, packed),
        [pltpu.SMEM] + [pltpu.VMEM] * 10,
        [
            pltpu.VMEM((25, 40, NZ), F32),
            pltpu.VMEM((17, 24, NZ), F32),
            pltpu.VMEM((25, 40, 256), F32),
            pltpu.VMEM((25, 40, 256), F32),
            pltpu.VMEM((18, 40, 256), F32),
            pltpu.VMEM((18, 32, 256), F32),
            pltpu.VMEM((CX + 1, 32, NZ), F32),
            pltpu.VMEM((4 * NZ, 2 * CX * CY), BF16),
        ],
    )
    return pot, force


def solution(mesh):
    return jax.shard_map(
        per_device,
        mesh=mesh,
        in_specs=(
            P("gx", "gy", None),
            P(None, "gx", "gy", None),
            P("gx", "gy", None),
            P("gx", "gy"),
            P(),
            P(),
            P(),
        ),
        out_specs=(P("gx", "gy", None), P(None, "gx", "gy", None)),
        check_vma=False,
    )
```
